32 devices in a mesh: ctx: 16 (over z, y, core), exp: 2 (over x).
Axes of the slice: x: 2, y: 2, z: 4, core: 2. Of those that a mesh axis runs over, the one named last changes fastest.
Arguments:
- hidden_in: bfloat16 [2, 3072, 1024], P('exp', 'ctx'), may hold values from -6 to 6
- queries: bfloat16 [2, 3072, 1024], P('exp', 'ctx'), may hold values from -128 to 128
- key_proj: bfloat16 [2, 3072, 256], P('exp', 'ctx'), may hold values from -16 to 16
- value_proj: bfloat16 [2, 3072, 256], P('exp', 'ctx'), may hold values from -6 to 6
- tile_mask: int32 [2, 96, 96], P('exp', 'ctx'), may hold values from 0 to 1, as said below
- out_weight: bfloat16 [1024, 1024], replicated, may hold values from -0.1875 to 0.1875
- moe_gain: float32 [1024], replicated, may hold values from 0.1 to 1.9
- gate_weight: bfloat16 [8, 1024, 1792], P('exp', 'ctx'), may hold values from -0.1875 to 0.1875
- up_weight: bfloat16 [8, 1024, 1792], P('exp', 'ctx'), may hold values from -0.1875 to 0.1875
- down_weight: bfloat16 [8, 1024, 1792], P('exp', 'ctx'), may hold values from -0.125 to 0.125
- expert_ids: int32 [2, 3072, 2], P('exp', 'ctx'), may hold values from 0 to 7, all different within a row; in each aligned block of 192 rows (0 to 191, 192 to 383, ..., all dimensions but the last counted through in order) at most 72 rows name the same one
- gate_probs: float32 [2, 3072, 2], P('exp', 'ctx'), may hold values from 0.05 to 0.95, as said below
Outputs:
- attention_out: bfloat16 [2, 3072, 1024], P('exp', 'ctx')
- layer_out: bfloat16 [2, 3072, 1024], P('exp', 'ctx')
The draws below stay inside these ranges and needn't reach their ends.
Inputs may be any that keep to these rules, and one draw needn't show every extreme that they name: `expert_ids`: within one block of 192 tokens of a sequence (the tokens of one device), no expert is named by more than 72 pairs; the 2 ids of a token differ. tile_mask[s, i, i] = 1 for every tile i. `gate_probs`: the 2 weights of a token sum to 1.
All inputs are finite; a program needn't handle non-finite values.
Results may differ from the reference program's by a relative error of at most 0.0065.
Values may be sent and summed in bfloat16 or wider, within the bound.
No kernel may reach another device: no remote copies, remote signals or barrier semaphores. Data moves between devices by JAX's collectives and lax.ppermute only.
A program may use at most 128 MiB of HBM per device.

```python
import math
import jax
import jax.numpy as jnp
import numpy as np
from jax import lax

D = 1024
HEADS = 8
KV_HEADS = 2
FF = 1792
EXPERTS = 8
TOP = 2
TILE = 32
TOK_DEV = 192
KVW = 256
SEQS = 2
LEN = 3072
NT = 96
CAP = 72
N_CTX = 16


def paired_keys(key):
    base = jax.random.normal(jax.random.fold_in(key, 11), (SEQS, LEN, KVW), jnp.float32)
    base = jnp.clip(base, -6.0, 6.0)
    return base


def draw_key_proj(key, part):
    return paired_keys(key).astype(jnp.bfloat16)


def draw_queries(key, part):
    base = jax.random.normal(jax.random.fold_in(key, 21), (SEQS, LEN, D), jnp.float32)
    base = jnp.clip(base, -6.0, 6.0)
    return base.astype(jnp.bfloat16)


def draw_tile_mask(key, part):
    density_level = jax.random.randint(jax.random.fold_in(key, 31), (SEQS, NT, 1), 1, 7)
    coin_draw = jax.random.randint(jax.random.fold_in(key, 32), (SEQS, NT, NT), 0, 128)
    tile_index = jnp.arange(NT)
    distance = jnp.abs(tile_index[:, None] - tile_index[None, :])
    on_diagonal = distance == 0
    near_band = distance <= 2
    near_on = near_band[None] & (coin_draw < 16 * density_level)
    far_on = jnp.logical_not(near_band)[None] & (coin_draw < 1)
    return jnp.where(on_diagonal[None] | near_on | far_on, 1, 0).astype(jnp.int32)


def draw_gate_probs(key, part):
    logit_gap = jnp.clip(jax.random.normal(jax.random.fold_in(key, 42), (SEQS, LEN, 1), jnp.float32), -2.9, 2.9)
    first = 1.0 / (1.0 + jnp.exp(-logit_gap))
    return jnp.concatenate([first, 1.0 - first], axis=2)


def block_scale(own_key, extent, shards, least, high):
    def one(axis_at, shards_of):
        draws = jax.random.uniform(jax.random.fold_in(jax.random.fold_in(own_key, 6), axis_at), (shards_of,), jnp.float32, least / len(shards), high / len(shards))
        return jnp.repeat(jnp.exp(draws), extent[axis_at] // shards_of).reshape((-1,) + (1,) * (len(extent) - axis_at - 1))

    factor_of = one(*shards[0])
    for cut in shards[1:]:
        factor_of = factor_of * one(*cut)
    return factor_of


def assign_block(stream_key, own, number, rows, amount, top, bound, lean):
    order = jax.random.permutation(stream_key, amount)
    packed, common = shares(amount, rows * top, bound, lean, True), shares(amount, rows * top, bound, lean, False)
    places = jnp.arange(amount)

    def named(tallies, offset_by):
        used = int((tallies > 0).sum())
        fixed = max(1, used // 4)
        moved = fixed + (places - fixed + offset_by * (used - fixed)) % max(1, amount - fixed)
        return jnp.zeros((amount,), jnp.int32).at[order[jnp.where(places < fixed, places, moved)]].set(jnp.asarray(tallies, jnp.int32))

    tallies = jnp.where(number % 4 == 0, named(packed, number // 4), named(common, number - number // 4 - 1))
    mixed = jax.random.permutation(jax.random.fold_in(own, 3), amount)
    donor, taker = mixed[0:amount // 2 * 2:2], mixed[1:amount // 2 * 2:2]
    slack = jnp.minimum(tallies[donor] - 1, bound - tallies[taker]) // 2
    slack = jnp.where((donor == order[0]) | (taker == order[0]) | (tallies[taker] == 0), 0, jnp.maximum(slack, 0))
    moved = jax.random.randint(jax.random.fold_in(own, 4), (amount // 2,), 0, 1 << 20) % (slack + 1)
    tallies = tallies.at[donor].add(-moved).at[taker].add(moved)
    labels = jnp.searchsorted(jnp.cumsum(tallies), jnp.arange(rows * top), side="right").astype(jnp.int32)
    listing = labels.reshape(top, rows).T
    listing = listing[jax.random.permutation(jax.random.fold_in(own, 1), rows)]
    offset_by = jax.random.randint(jax.random.fold_in(own, 2), (rows, 1), 0, top)
    return jnp.take_along_axis(listing, (jnp.arange(top)[None, :] + offset_by) % top, axis=1)


def shares(amount, total, most, slope, full):
    loads = [(1 << 20) // math.isqrt(rank ** slope) + 1 for rank in range(1, amount + 1)]
    largest = most if full else min(most, max(-(-total // amount), total * loads[0] // sum(loads)))
    least = 1 if total - largest >= amount - 1 else 0
    counts, surplus = [largest] + [least] * (amount - 1), total - largest - least * (amount - 1)
    while surplus > 0:
        free = [i for i in range(1, amount) if counts[i] < largest] or [i for i in range(1, amount) if counts[i] < most]
        mass, remaining = sum([loads[i] for i in free]), surplus
        for i in free:
            extra = min(most - counts[i], max(1, remaining * loads[i] // mass), surplus)
            counts[i] = counts[i] + extra
            surplus = surplus - extra
    return np.array(counts)


def scatter_about(key, extent, spread, reach, split=(), kind=jnp.bfloat16):
    values = jax.random.normal(key, extent, jnp.float32) * spread
    if len(split) > 0:
        values = block_scale(key, extent, split, -0.22, 0.18) * values
    return jnp.clip(values, min=-reach, max=reach).astype(kind)


def setup_inputs(seed: int = 0) -> dict:
    key_of = jax.random.split(jax.random.key(seed), 13)
    hidden_in = scatter_about(key_of[0], (SEQS, LEN, D), 1.0, 6.0, ((0, 2), (1, 16)))
    queries = draw_queries(jax.random.fold_in(key_of[12], 71), 0)
    key_proj = draw_key_proj(jax.random.fold_in(key_of[12], 71), 0)
    value_proj = scatter_about(key_of[3], (SEQS, LEN, KVW), 1.0, 6.0, ((0, 2), (1, 16)))
    tile_mask = draw_tile_mask(jax.random.fold_in(key_of[12], 71), 0)
    out_weight = scatter_about(key_of[5], (D, D), D ** -0.5, 0.1875)
    moe_gain = jnp.clip(1.0 + 0.18 * jax.random.normal(key_of[6], (D,), jnp.float32), 0.1, 1.9)
    gate_weight = scatter_about(key_of[7], (EXPERTS, D, FF), D ** -0.5, 0.1875, ((0, 2), (1, 16)))
    up_weight = scatter_about(key_of[8], (EXPERTS, D, FF), D ** -0.5, 0.1875, ((0, 2), (1, 16)))
    down_weight = scatter_about(key_of[9], (EXPERTS, D, FF), FF ** -0.5, 0.125, ((0, 2), (1, 16)))
    expert_ids_keys = jax.random.split(jax.random.fold_in(key_of[10], 1), SEQS * LEN // TOK_DEV)
    expert_ids_turns = jax.random.permutation(jax.random.fold_in(key_of[10], 3), SEQS * LEN // TOK_DEV)
    expert_ids = jax.vmap(lambda own, number: assign_block(jax.random.fold_in(key_of[10], 2), own, number, TOK_DEV, EXPERTS, TOP, CAP, 2))(expert_ids_keys, expert_ids_turns).reshape((SEQS, LEN, TOP))
    gate_probs = draw_gate_probs(jax.random.fold_in(key_of[12], 71), 0)
    return dict(hidden_in=hidden_in, queries=queries, key_proj=key_proj, value_proj=value_proj, tile_mask=tile_mask, out_weight=out_weight, moe_gain=moe_gain, gate_weight=gate_weight, up_weight=up_weight, down_weight=down_weight, expert_ids=expert_ids, gate_probs=gate_probs)


def rms_scale(row_block, gain):
    widened = row_block.astype(jnp.float32)
    inverse = lax.rsqrt(lax.optimization_barrier(jnp.mean(widened * widened, axis=-1, keepdims=True)) + 1e-05)
    return widened * inverse * gain.astype(jnp.float32)

def attend_block(query_rows, key_rows, value_rows, mask_rows):
    row_count = query_rows.shape[0]
    groups = HEADS // KV_HEADS
    head_size = D // HEADS
    query_heads = query_rows.reshape(row_count, KV_HEADS, groups, head_size).astype(jnp.float32)
    key_heads = key_rows.reshape(-1, KV_HEADS, head_size).astype(jnp.float32)
    value_heads = value_rows.reshape(-1, KV_HEADS, head_size).astype(jnp.float32)
    scores = jnp.einsum('qkgd,rkd->kgqr', query_heads, key_heads) * head_size ** (-0.5)
    allowed = jnp.repeat(jnp.repeat(mask_rows, TILE, axis=0), TILE, axis=1) > 0
    scores = jnp.where(allowed, scores, -1e+30)
    highest = lax.optimization_barrier(jnp.max(scores, axis=-1, keepdims=True))
    weights = jnp.where(allowed, jnp.exp(scores - highest), 0.0)
    denominator = lax.optimization_barrier(jnp.sum(weights, axis=-1, keepdims=True))
    rounded = lax.optimization_barrier(weights.astype(jnp.bfloat16))
    attended = jnp.einsum('kgqr,rkd->kgqd', rounded.astype(jnp.float32), value_heads) / denominator
    return attended.transpose(2, 0, 1, 3).reshape(row_count, D).astype(jnp.bfloat16)

def slot_rank(id_row):
    onehot = (id_row[:, None] == jnp.arange(EXPERTS, dtype=jnp.int32)[None, :]).astype(jnp.int32)
    before = jnp.cumsum(onehot, axis=0) - onehot
    return lax.optimization_barrier(jnp.sum(before * onehot, axis=1)).astype(jnp.int32)

def fill_slots(row_block, id_row, slot_row):
    repeated = jnp.repeat(row_block, TOP, axis=0)
    return jnp.zeros((EXPERTS, CAP, D), jnp.bfloat16).at[id_row, slot_row].set(repeated)

def run_expert(bundle):
    slot_rows, gate_w, up_w, down_w = bundle
    gated = jnp.dot(slot_rows, gate_w, preferred_element_type=jnp.float32)
    up_values = jnp.dot(slot_rows, up_w, preferred_element_type=jnp.float32)
    hidden = (jax.nn.silu(gated) * up_values).astype(jnp.bfloat16)
    return jnp.dot(hidden, down_w.T, preferred_element_type=jnp.float32).astype(jnp.bfloat16)

def reference(hidden_in, queries, key_proj, value_proj, tile_mask, out_weight, moe_gain, gate_weight, up_weight, down_weight, expert_ids, gate_probs):

    def one_sequence(bundle):
        query_seq, key_seq, value_seq, mask_seq = bundle
        query_blocks = query_seq.reshape(N_CTX, TOK_DEV, D)
        mask_blocks = mask_seq.reshape(N_CTX, TOK_DEV // TILE, NT)

        def one_block(couple):
            return attend_block(couple[0], key_seq, value_seq, couple[1])
        return lax.map(one_block, (query_blocks, mask_blocks)).reshape(LEN, D)
    attended = lax.map(one_sequence, (queries, key_proj, value_proj, tile_mask))
    projected = jnp.dot(attended.reshape(-1, D), out_weight, preferred_element_type=jnp.float32)
    attention_out = projected.astype(jnp.bfloat16).reshape(SEQS, LEN, D)
    residual = (hidden_in.reshape(-1, D).astype(jnp.float32) + projected).astype(jnp.bfloat16)
    normed = rms_scale(residual, moe_gain).astype(jnp.bfloat16)
    block_count = SEQS * N_CTX
    row_blocks = normed.reshape(block_count, TOK_DEV, D)
    id_rows = expert_ids.reshape(block_count, TOK_DEV * TOP).astype(jnp.int32)
    slot_rows = jax.vmap(slot_rank)(id_rows)
    buffers = jax.vmap(fill_slots)(row_blocks, id_rows, slot_rows)
    per_expert = jnp.moveaxis(buffers, 1, 0).reshape(EXPERTS, block_count * CAP, D)
    outputs = lax.map(run_expert, (per_expert, gate_weight, up_weight, down_weight))
    outputs = jnp.moveaxis(outputs.reshape(EXPERTS, block_count, CAP, D), 0, 1).reshape(block_count, EXPERTS * CAP, D)

    def pick_rows(output_block, id_row, slot_row):
        return jnp.take(output_block, id_row * CAP + slot_row, axis=0)
    picked = jax.vmap(pick_rows)(outputs, id_rows, slot_rows).reshape(block_count, TOK_DEV, TOP, D)
    probs = gate_probs.reshape(block_count, TOK_DEV, TOP).astype(jnp.float32)
    mixture = lax.optimization_barrier(jnp.sum(picked.astype(jnp.float32) * probs[..., None], axis=2))
    layer_out = (residual.reshape(block_count, TOK_DEV, D).astype(jnp.float32) + mixture).astype(jnp.bfloat16)
    return (attention_out, layer_out.reshape(SEQS, LEN, D))
```

```python
import functools

import jax
import jax.numpy as jnp
from jax import lax
from jax.experimental import pallas as pl
from jax.experimental.pallas import tpu as pltpu
from jax.sharding import Mesh, PartitionSpec as P

D = 1024
HEADS = 8
KV_HEADS = 2
EXPERTS = 8
TOP = 2
TILE = 32
CAP = 72
HEAD = D // HEADS
GROUPS = HEADS // KV_HEADS
KVW = KV_HEADS * HEAD
SLOTS = EXPERTS * CAP
MB = 1 << 20

VMEM = pl.BlockSpec(memory_space=pltpu.VMEM)
SMEM = pl.BlockSpec(memory_space=pltpu.SMEM)
ANY = pl.BlockSpec(memory_space=pl.ANY)


def pack_kernel(planes, place_ref, gate_ref, up_ref, down_ref, *rest):
    outs, sems = rest[:planes], rest[planes]
    plane = place_ref[0]
    copies = []
    for k in range(planes):
        owner = plane ^ k
        for w, ref in enumerate((gate_ref, up_ref, down_ref)):
            copies.append(pltpu.make_async_copy(ref.at[owner], outs[k].at[w], sems.at[3 * k + w]))
    for copy in copies:
        copy.start()
    for copy in copies:
        copy.wait()


def pack(place, gate, up, down):
    planes, rows, ff = gate.shape
    return pl.pallas_call(
        functools.partial(pack_kernel, planes),
        out_shape=[jax.ShapeDtypeStruct((3, rows, ff), gate.dtype)] * planes,
        in_specs=[SMEM, ANY, ANY, ANY],
        out_specs=[ANY] * planes,
        scratch_shapes=[pltpu.SemaphoreType.DMA((3 * planes,))],
        name="pack_weights",
    )(place, gate, up, down)


def attend_kernel(blocks, chunk, live_ref, query_ref, bias_ref, target_ref, out_w_ref, hidden_ref, gain_ref, *rest):
    kv_refs = rest[:blocks]
    attention_ref, residual_ref, outgoing_ref, kv, scores, top, total, acc, attended = rest[blocks:]
    rows = query_ref.shape[0]
    chunks = scores.shape[0]
    for i in range(blocks):
        kv[pl.ds(i * rows, rows), :] = kv_refs[i][...]
    scale = HEAD ** (-0.5)
    for h in range(KV_HEADS):
        heads = [query_ref[:, (h * GROUPS + g) * HEAD : (h * GROUPS + g + 1) * HEAD] for g in range(GROUPS)]
        query = jnp.concatenate(heads, axis=0)
        top[...] = jnp.full(top.shape, -1e30, jnp.float32)
        total[...] = jnp.zeros(total.shape, jnp.float32)
        acc[...] = jnp.zeros(acc.shape, jnp.float32)

        @pl.loop(0, chunks)
        def _(j):
            @pl.when(live_ref[j] > 0)
            def _():
                keys = kv[pl.ds(pl.multiple_of(j * chunk, 128), chunk), h * HEAD : (h + 1) * HEAD]
                s = lax.dot_general(query, keys, (((1,), (1,)), ((), ())), preferred_element_type=jnp.float32)
                s = s.reshape(GROUPS, rows, chunk) + bias_ref[j][None]
                s = s.reshape(GROUPS * rows, chunk)
                scores[j] = s
                best = top[...]
                for c in range(0, chunk, 128):
                    best = jnp.maximum(best, s[:, c : c + 128])
                top[...] = best

        highest = jnp.max(top[...], axis=1, keepdims=True)
        top[...] = jnp.broadcast_to(highest, top.shape)

        @pl.loop(0, chunks)
        def _(j):
            @pl.when(live_ref[j] > 0)
            def _():
                values = kv[pl.ds(pl.multiple_of(j * chunk, 128), chunk), KVW + h * HEAD : KVW + (h + 1) * HEAD]
                high = top[...]
                s = scores[j]
                parts = []
                running = total[...]
                for c in range(0, chunk, 128):
                    w = jnp.exp((s[:, c : c + 128] - high) * scale)
                    running = running + w
                    parts.append(w.astype(jnp.bfloat16))
                total[...] = running
                weights = jnp.concatenate(parts, axis=1)
                acc[...] += jnp.dot(weights, values, preferred_element_type=jnp.float32)

        denominator = jnp.sum(total[...], axis=1, keepdims=True)
        result = (acc[...] / denominator).astype(jnp.bfloat16)
        for g in range(GROUPS):
            col = (h * GROUPS + g) * HEAD
            attended[:, col : col + HEAD] = result[g * rows : (g + 1) * rows]
    projected = jnp.dot(attended[...], out_w_ref[...], preferred_element_type=jnp.float32)
    attention_ref[...] = projected.astype(jnp.bfloat16)
    residual = (hidden_ref[...].astype(jnp.float32) + projected).astype(jnp.bfloat16)
    residual_ref[...] = residual
    wide = residual.astype(jnp.float32)
    inverse = lax.rsqrt(jnp.mean(wide * wide, axis=-1, keepdims=True) + 1e-05)
    normed = (wide * inverse * gain_ref[...]).astype(jnp.bfloat16)
    slot = lax.broadcasted_iota(jnp.int32, (SLOTS, rows), 0)
    chosen = (slot == target_ref[0:1, :]) | (slot == target_ref[1:2, :])
    selector = chosen.astype(jnp.float32).astype(jnp.bfloat16)
    outgoing_ref[...] = jnp.dot(selector, normed, preferred_element_type=jnp.float32).astype(jnp.bfloat16)


def attend(live, query, bias, target, out_w, hidden, gain, blocks):
    rows = query.shape[0]
    chunks, _, chunk = bias.shape
    n = len(blocks)
    return pl.pallas_call(
        functools.partial(attend_kernel, n, chunk),
        out_shape=[
            jax.ShapeDtypeStruct((rows, D), jnp.bfloat16),
            jax.ShapeDtypeStruct((rows, D), jnp.bfloat16),
            jax.ShapeDtypeStruct((SLOTS, D), jnp.bfloat16),
        ],
        in_specs=[SMEM] + [VMEM] * (6 + n),
        out_specs=[VMEM] * 3,
        scratch_shapes=[
            pltpu.VMEM((n * rows, 2 * KVW), jnp.bfloat16),
            pltpu.VMEM((chunks, GROUPS * rows, chunk), jnp.float32),
            pltpu.VMEM((GROUPS * rows, HEAD), jnp.float32),
            pltpu.VMEM((GROUPS * rows, HEAD), jnp.float32),
            pltpu.VMEM((GROUPS * rows, HEAD), jnp.float32),
            pltpu.VMEM((rows, D), jnp.bfloat16),
        ],
        compiler_params=pltpu.CompilerParams(vmem_limit_bytes=48 * MB),
        name="attend",
    )(live, query, bias, target, out_w, hidden, gain, *blocks)


def expert_kernel(planes, shared, place_ref, rows_ref, *rest):
    count = planes * shared
    pieces = rest[:count]
    out_ref, gate, up, down, total, sems = rest[count:]
    depth, ff = pieces[0].shape[1:]
    plane, seat = place_ref[0], place_ref[1]
    copies = [[], [], []]
    for w, full in enumerate((gate, up, down)):
        for m in range(shared):
            for k in range(planes):
                at = ((plane ^ k) * shared + (seat ^ m)) * depth
                target = full.at[pl.ds(pl.multiple_of(at, depth), depth), :]
                n = m * planes + k
                copies[w].append(pltpu.make_async_copy(pieces[n].at[w], target, sems.at[w * count + n]))
    for group in copies:
        for copy in group:
            copy.start()
    for group in copies[:2]:
        for copy in group:
            copy.wait()
    step = 256
    for n, c in enumerate(range(0, ff, step)):
        rows = rows_ref[...]
        gated = jnp.dot(rows, gate[:, c : c + step], preferred_element_type=jnp.float32)
        upper = jnp.dot(rows, up[:, c : c + step], preferred_element_type=jnp.float32)
        hidden = (gated / (1.0 + jnp.exp(-gated)) * upper).astype(jnp.bfloat16)
        if n == 0:
            for copy in copies[2]:
                copy.wait()
        part = lax.dot_general(
            hidden, down[:, c : c + step], (((1,), (1,)), ((), ())), preferred_element_type=jnp.float32
        )
        if n == 0:
            total[...] = part
        else:
            total[...] += part
    out_ref[...] = total[...].astype(jnp.bfloat16)


def run_expert(place, rows, pieces, planes, shared):
    depth, ff = pieces[0].shape[1:]
    count = planes * shared
    return pl.pallas_call(
        functools.partial(expert_kernel, planes, shared),
        out_shape=jax.ShapeDtypeStruct(rows.shape, jnp.bfloat16),
        in_specs=[SMEM, VMEM] + [ANY] * count,
        out_specs=VMEM,
        scratch_shapes=[
            pltpu.VMEM((D, ff), jnp.bfloat16),
            pltpu.VMEM((D, ff), jnp.bfloat16),
            pltpu.VMEM((D, ff), jnp.bfloat16),
            pltpu.VMEM(rows.shape, jnp.float32),
            pltpu.SemaphoreType.DMA((3 * count,)),
        ],
        compiler_params=pltpu.CompilerParams(vmem_limit_bytes=48 * MB),
        name="expert",
    )(place, rows, *pieces)


def combine_kernel(returned_ref, target_ref, probs_ref, residual_ref, out_ref):
    rows = residual_ref.shape[0]
    slot = lax.broadcasted_iota(jnp.int32, (rows, SLOTS), 1)
    returned = returned_ref[...]
    total = jnp.zeros((rows, D), jnp.float32)
    for k in range(TOP):
        selector = (slot == target_ref[:, k : k + 1]).astype(jnp.float32).astype(jnp.bfloat16)
        picked = jnp.dot(selector, returned, preferred_element_type=jnp.float32)
        total = total + picked * probs_ref[:, k : k + 1]
    out_ref[...] = (residual_ref[...].astype(jnp.float32) + total).astype(jnp.bfloat16)


def combine(returned, target, probs, residual):
    return pl.pallas_call(
        combine_kernel,
        out_shape=jax.ShapeDtypeStruct(residual.shape, jnp.bfloat16),
        in_specs=[VMEM] * 4,
        out_specs=VMEM,
        compiler_params=pltpu.CompilerParams(vmem_limit_bytes=32 * MB),
        name="combine",
    )(returned, target, probs, residual)


def slots_of(ids):
    rows = ids.shape[0]
    onehot = (ids[:, :, None] == jnp.arange(EXPERTS, dtype=jnp.int32)).astype(jnp.float32)
    named = jnp.sum(onehot, axis=1)
    earlier = (jnp.arange(rows)[:, None] > jnp.arange(rows)[None, :]).astype(jnp.bfloat16)
    before = jnp.dot(earlier, named.astype(jnp.bfloat16), preferred_element_type=jnp.float32)
    slot = jnp.sum(onehot * before[:, None, :], axis=2).astype(jnp.int32)
    return ids * CAP + slot


def shards(
    planes,
    shared,
    hidden_in,
    queries,
    key_proj,
    value_proj,
    tile_mask,
    out_weight,
    moe_gain,
    gate_weight,
    up_weight,
    down_weight,
    expert_ids,
    gate_probs,
):
    ctx = ("plane", "seat")
    world = planes * shared
    rows = queries.shape[1]
    tiles = rows // TILE
    plane = lax.axis_index("plane")
    seat = lax.axis_index("seat")
    me = plane * shared + seat
    place = jnp.stack([plane, seat]).astype(jnp.int32)

    def swap(x, bit):
        return lax.ppermute(x, ctx, [(i, i ^ bit) for i in range(world)])

    blocks = {0: jnp.concatenate([key_proj[0], value_proj[0]], axis=1)}
    bit = world // 2
    while bit:
        blocks.update({m | bit: swap(x, bit) for m, x in list(blocks.items())})
        bit //= 2
    packed = pack(place, gate_weight, up_weight, down_weight)
    pieces = {(0, 0): packed[0]}
    for k in range(1, planes):
        pieces[0, k] = swap(packed[k], k * shared)
    bit = shared // 2
    while bit:
        pieces.update({(m | bit, k): swap(x, bit) for (m, k), x in list(pieces.items())})
        bit //= 2

    target = slots_of(expert_ids[0])
    chunk = 2 * rows
    order = me ^ jnp.arange(world)
    mask = jnp.take(tile_mask[0].reshape(tiles, world, tiles), order, axis=1)
    mask = mask.reshape(tiles, world // 2, 2 * tiles).transpose(1, 0, 2)
    live = jnp.max(mask, axis=(1, 2)).astype(jnp.int32)
    bias = jnp.where(mask > 0, 0.0, -1e30).astype(jnp.float32)
    bias = jnp.repeat(jnp.repeat(bias, TILE, axis=1), TILE, axis=2)

    attention_out, residual, outgoing = attend(
        live,
        queries[0],
        bias,
        target.T,
        out_weight,
        hidden_in[0],
        moe_gain[None],
        [blocks[m] for m in range(world)],
    )
    arrived = lax.all_to_all(
        outgoing.reshape(EXPERTS, CAP, D), ("exp", "plane"), split_axis=0, concat_axis=0, tiled=True
    )
    expert_rows = run_expert(
        place,
        arrived.reshape(SLOTS, D),
        [pieces[m, k] for m in range(shared) for k in range(planes)],
        planes,
        shared,
    )
    returned = lax.all_to_all(
        expert_rows.reshape(EXPERTS, CAP, D), ("exp", "plane"), split_axis=0, concat_axis=0, tiled=True
    )
    layer_out = combine(returned.reshape(SLOTS, D), target, gate_probs[0], residual)
    return attention_out[None], layer_out[None]


def solution(mesh):
    n_ctx, n_exp = mesh.shape["ctx"], mesh.shape["exp"]
    planes = EXPERTS // n_exp
    shared = n_ctx // planes
    fine = Mesh(mesh.devices.reshape(planes, shared, n_exp), ("plane", "seat", "exp"))
    split = P("exp", ("plane", "seat"), None)
    return jax.shard_map(
        functools.partial(shards, planes, shared),
        mesh=fine,
        in_specs=(split, split, split, split, split, P(), P(), split, split, split, split, split),
        out_specs=(split, split),
        check_vma=False,
    )
```

```python
import functools

import jax
import jax.numpy as jnp
from jax import lax
from jax.experimental import pallas as pl
from jax.experimental.pallas import tpu as pltpu
from jax.sharding import Mesh, PartitionSpec as P

D = 1024
HEADS = 8
KV_HEADS = 2
EXPERTS = 8
TOP = 2
TILE = 32
CAP = 72
HEAD = D // HEADS
GROUPS = HEADS // KV_HEADS
KVW = KV_HEADS * HEAD
SLOTS = EXPERTS * CAP
MB = 1 << 20

VMEM = pl.BlockSpec(memory_space=pltpu.VMEM)
SMEM = pl.BlockSpec(memory_space=pltpu.SMEM)
ANY = pl.BlockSpec(memory_space=pl.ANY)


def pack_kernel(planes, place_ref, gate_ref, up_ref, down_ref, *rest):
    outs, sems = rest[:planes], rest[planes]
    plane = place_ref[0]
    copies = []
    for k in range(planes):
        owner = plane ^ k
        for w, ref in enumerate((gate_ref, up_ref, down_ref)):
            copies.append(pltpu.make_async_copy(ref.at[owner], outs[k].at[w], sems.at[3 * k + w]))
    for copy in copies:
        copy.start()
    for copy in copies:
        copy.wait()


def pack(place, gate, up, down):
    planes, rows, ff = gate.shape
    return pl.pallas_call(
        functools.partial(pack_kernel, planes),
        out_shape=[jax.ShapeDtypeStruct((3, rows, ff), gate.dtype)] * planes,
        in_specs=[SMEM, ANY, ANY, ANY],
        out_specs=[VMEM] * planes,
        scratch_shapes=[pltpu.SemaphoreType.DMA((3 * planes,))],
        name="pack_weights",
    )(place, gate, up, down)


def attend_kernel(blocks, chunk, live_ref, query_ref, bias_ref, target_ref, out_w_ref, hidden_ref, gain_ref, *rest):
    kv_refs = rest[:blocks]
    attention_ref, residual_ref, outgoing_ref, kv, scores, top, total, acc, attended = rest[blocks:]
    rows = query_ref.shape[0]
    chunks = scores.shape[0]
    for i in range(blocks):
        kv[pl.ds(i * rows, rows), :] = kv_refs[i][...]
    scale = HEAD ** (-0.5)
    for h in range(KV_HEADS):
        heads = [query_ref[:, (h * GROUPS + g) * HEAD : (h * GROUPS + g + 1) * HEAD] for g in range(GROUPS)]
        query = jnp.concatenate(heads, axis=0)
        top[...] = jnp.full(top.shape, -1e30, jnp.float32)
        total[...] = jnp.zeros(total.shape, jnp.float32)
        acc[...] = jnp.zeros(acc.shape, jnp.float32)

        @pl.loop(0, chunks)
        def _(j):
            @pl.when(live_ref[j] > 0)
            def _():
                keys = kv[pl.ds(pl.multiple_of(j * chunk, 128), chunk), h * HEAD : (h + 1) * HEAD]
                s = lax.dot_general(query, keys, (((1,), (1,)), ((), ())), preferred_element_type=jnp.float32)
                s = s.reshape(GROUPS, rows, chunk) + bias_ref[j][None]
                s = s.reshape(GROUPS * rows, chunk)
                scores[j] = s
                best = top[...]
                for c in range(0, chunk, 128):
                    best = jnp.maximum(best, s[:, c : c + 128])
                top[...] = best

        highest = jnp.max(top[...], axis=1, keepdims=True)
        top[...] = jnp.broadcast_to(highest, top.shape)

        @pl.loop(0, chunks)
        def _(j):
            @pl.when(live_ref[j] > 0)
            def _():
                values = kv[pl.ds(pl.multiple_of(j * chunk, 128), chunk), KVW + h * HEAD : KVW + (h + 1) * HEAD]
                high = top[...]
                s = scores[j]
                parts = []
                running = total[...]
                for c in range(0, chunk, 128):
                    w = jnp.exp((s[:, c : c + 128] - high) * scale)
                    running = running + w
                    parts.append(w.astype(jnp.bfloat16))
                total[...] = running
                weights = jnp.concatenate(parts, axis=1)
                acc[...] += jnp.dot(weights, values, preferred_element_type=jnp.float32)

        denominator = jnp.sum(total[...], axis=1, keepdims=True)
        result = (acc[...] / denominator).astype(jnp.bfloat16)
        for g in range(GROUPS):
            col = (h * GROUPS + g) * HEAD
            attended[:, col : col + HEAD] = result[g * rows : (g + 1) * rows]
    projected = jnp.dot(attended[...], out_w_ref[...], preferred_element_type=jnp.float32)
    attention_ref[...] = projected.astype(jnp.bfloat16)
    residual = (hidden_ref[...].astype(jnp.float32) + projected).astype(jnp.bfloat16)
    residual_ref[...] = residual
    wide = residual.astype(jnp.float32)
    inverse = lax.rsqrt(jnp.mean(wide * wide, axis=-1, keepdims=True) + 1e-05)
    normed = (wide * inverse * gain_ref[...]).astype(jnp.bfloat16)
    slot = lax.broadcasted_iota(jnp.int32, (SLOTS, rows), 0)
    chosen = (slot == target_ref[0:1, :]) | (slot == target_ref[1:2, :])
    selector = chosen.astype(jnp.float32).astype(jnp.bfloat16)
    outgoing_ref[...] = jnp.dot(selector, normed, preferred_element_type=jnp.float32).astype(jnp.bfloat16)


def attend(live, query, bias, target, out_w, hidden, gain, blocks):
    rows = query.shape[0]
    chunks, _, chunk = bias.shape
    n = len(blocks)
    return pl.pallas_call(
        functools.partial(attend_kernel, n, chunk),
        out_shape=[
            jax.ShapeDtypeStruct((rows, D), jnp.bfloat16),
            jax.ShapeDtypeStruct((rows, D), jnp.bfloat16),
            jax.ShapeDtypeStruct((SLOTS, D), jnp.bfloat16),
        ],
        in_specs=[SMEM] + [VMEM] * (6 + n),
        out_specs=[VMEM] * 3,
        scratch_shapes=[
            pltpu.VMEM((n * rows, 2 * KVW), jnp.bfloat16),
            pltpu.VMEM((chunks, GROUPS * rows, chunk), jnp.float32),
            pltpu.VMEM((GROUPS * rows, HEAD), jnp.float32),
            pltpu.VMEM((GROUPS * rows, HEAD), jnp.float32),
            pltpu.VMEM((GROUPS * rows, HEAD), jnp.float32),
            pltpu.VMEM((rows, D), jnp.bfloat16),
        ],
        compiler_params=pltpu.CompilerParams(vmem_limit_bytes=48 * MB),
        name="attend",
    )(live, query, bias, target, out_w, hidden, gain, *blocks)


def expert_kernel(planes, shared, place_ref, rows_ref, *rest):
    count = planes * shared
    pieces = rest[:count]
    out_ref, gate, up, down, total, sems = rest[count:]
    depth, ff = pieces[0].shape[1:]
    plane, seat = place_ref[0], place_ref[1]
    copies = [[], [], []]
    for w, full in enumerate((gate, up, down)):
        for m in range(shared):
            for k in range(planes):
                at = ((plane ^ k) * shared + (seat ^ m)) * depth
                target = full.at[pl.ds(pl.multiple_of(at, depth), depth), :]
                n = m * planes + k
                copies[w].append(pltpu.make_async_copy(pieces[n].at[w], target, sems.at[w * count + n]))
    for group in copies:
        for copy in group:
            copy.start()
    for group in copies[:2]:
        for copy in group:
            copy.wait()
    step = 256
    for n, c in enumerate(range(0, ff, step)):
        rows = rows_ref[...]
        gated = jnp.dot(rows, gate[:, c : c + step], preferred_element_type=jnp.float32)
        upper = jnp.dot(rows, up[:, c : c + step], preferred_element_type=jnp.float32)
        hidden = (gated / (1.0 + jnp.exp(-gated)) * upper).astype(jnp.bfloat16)
        if n == 0:
            for copy in copies[2]:
                copy.wait()
        part = lax.dot_general(
            hidden, down[:, c : c + step], (((1,), (1,)), ((), ())), preferred_element_type=jnp.float32
        )
        if n == 0:
            total[...] = part
        else:
            total[...] += part
    out_ref[...] = total[...].astype(jnp.bfloat16)


def run_expert(place, rows, pieces, planes, shared):
    depth, ff = pieces[0].shape[1:]
    count = planes * shared
    return pl.pallas_call(
        functools.partial(expert_kernel, planes, shared),
        out_shape=jax.ShapeDtypeStruct(rows.shape, jnp.bfloat16),
        in_specs=[SMEM, VMEM] + [ANY] * count,
        out_specs=VMEM,
        scratch_shapes=[
            pltpu.VMEM((D, ff), jnp.bfloat16),
            pltpu.VMEM((D, ff), jnp.bfloat16),
            pltpu.VMEM((D, ff), jnp.bfloat16),
            pltpu.VMEM(rows.shape, jnp.float32),
            pltpu.SemaphoreType.DMA((3 * count,)),
        ],
        compiler_params=pltpu.CompilerParams(vmem_limit_bytes=48 * MB),
        name="expert",
    )(place, rows, *pieces)


def combine_kernel(returned_ref, target_ref, probs_ref, residual_ref, out_ref):
    rows = residual_ref.shape[0]
    slot = lax.broadcasted_iota(jnp.int32, (rows, SLOTS), 1)
    returned = returned_ref[...]
    total = jnp.zeros((rows, D), jnp.float32)
    for k in range(TOP):
        selector = (slot == target_ref[:, k : k + 1]).astype(jnp.float32).astype(jnp.bfloat16)
        picked = jnp.dot(selector, returned, preferred_element_type=jnp.float32)
        total = total + picked * probs_ref[:, k : k + 1]
    out_ref[...] = (residual_ref[...].astype(jnp.float32) + total).astype(jnp.bfloat16)


def combine(returned, target, probs, residual):
    return pl.pallas_call(
        combine_kernel,
        out_shape=jax.ShapeDtypeStruct(residual.shape, jnp.bfloat16),
        in_specs=[VMEM] * 4,
        out_specs=VMEM,
        compiler_params=pltpu.CompilerParams(vmem_limit_bytes=32 * MB),
        name="combine",
    )(returned, target, probs, residual)


def slots_of(ids):
    rows = ids.shape[0]
    onehot = (ids[:, :, None] == jnp.arange(EXPERTS, dtype=jnp.int32)).astype(jnp.float32)
    named = jnp.sum(onehot, axis=1)
    earlier = (jnp.arange(rows)[:, None] > jnp.arange(rows)[None, :]).astype(jnp.bfloat16)
    before = jnp.dot(earlier, named.astype(jnp.bfloat16), preferred_element_type=jnp.float32)
    slot = jnp.sum(onehot * before[:, None, :], axis=2).astype(jnp.int32)
    return ids * CAP + slot


def shards(
    planes,
    shared,
    hidden_in,
    queries,
    key_proj,
    value_proj,
    tile_mask,
    out_weight,
    moe_gain,
    gate_weight,
    up_weight,
    down_weight,
    expert_ids,
    gate_probs,
):
    ctx = ("plane", "seat")
    world = planes * shared
    rows = queries.shape[1]
    tiles = rows // TILE
    plane = lax.axis_index("plane")
    seat = lax.axis_index("seat")
    me = plane * shared + seat
    place = jnp.stack([plane, seat]).astype(jnp.int32)

    def swap(x, bit):
        return lax.ppermute(x, ctx, [(i, i ^ bit) for i in range(world)])

    blocks = {0: jnp.concatenate([key_proj[0], value_proj[0]], axis=1)}
    packed = pack(place, gate_weight, up_weight, down_weight)
    bit = world // 2
    while bit:
        blocks.update({m | bit: swap(x, bit) for m, x in list(blocks.items())})
        if bit == world // 2:
            blocks, packed = lax.optimization_barrier((blocks, packed))
        bit //= 2
    pieces = {(0, 0): packed[0]}
    for k in range(1, planes):
        pieces[0, k] = swap(packed[k], k * shared)
    bit = shared // 2
    while bit:
        pieces.update({(m | bit, k): swap(x, bit) for (m, k), x in list(pieces.items())})
        bit //= 2

    target = slots_of(expert_ids[0])
    chunk = 2 * rows
    order = me ^ jnp.arange(world)
    mask = jnp.take(tile_mask[0].reshape(tiles, world, tiles), order, axis=1)
    mask = mask.reshape(tiles, world // 2, 2 * tiles).transpose(1, 0, 2)
    live = jnp.max(mask, axis=(1, 2)).astype(jnp.int32)
    bias = jnp.where(mask > 0, 0.0, -1e30).astype(jnp.float32)
    bias = jnp.repeat(jnp.repeat(bias, TILE, axis=1), TILE, axis=2)

    attention_out, residual, outgoing = attend(
        live,
        queries[0],
        bias,
        target.T,
        out_weight,
        hidden_in[0],
        moe_gain[None],
        [blocks[m] for m in range(world)],
    )
    arrived = lax.all_to_all(
        outgoing.reshape(EXPERTS, CAP, D), ("exp", "plane"), split_axis=0, concat_axis=0, tiled=True
    )
    expert_rows = run_expert(
        place,
        arrived.reshape(SLOTS, D),
        [pieces[m, k] for m in range(shared) for k in range(planes)],
        planes,
        shared,
    )
    returned = lax.all_to_all(
        expert_rows.reshape(EXPERTS, CAP, D), ("exp", "plane"), split_axis=0, concat_axis=0, tiled=True
    )
    layer_out = combine(returned.reshape(SLOTS, D), target, gate_probs[0], residual)
    return attention_out[None], layer_out[None]


def solution(mesh):
    n_ctx, n_exp = mesh.shape["ctx"], mesh.shape["exp"]
    planes = EXPERTS // n_exp
    shared = n_ctx // planes
    fine = Mesh(mesh.devices.reshape(planes, shared, n_exp), ("plane", "seat", "exp"))
    split = P("exp", ("plane", "seat"), None)
    return jax.shard_map(
        functools.partial(shards, planes, shared),
        mesh=fine,
        in_specs=(split, split, split, split, split, P(), P(), split, split, split, split, split),
        out_specs=(split, split),
        check_vma=False,
    )
```

```python
import functools

import jax
import jax.numpy as jnp
from jax import lax
from jax.experimental import pallas as pl
from jax.experimental.pallas import tpu as pltpu
from jax.sharding import Mesh, PartitionSpec as P

D = 1024
HEADS = 8
KV_HEADS = 2
EXPERTS = 8
TOP = 2
TILE = 32
CAP = 72
HEAD = D // HEADS
GROUPS = HEADS // KV_HEADS
KVW = KV_HEADS * HEAD
SLOTS = EXPERTS * CAP
MB = 1 << 20

VMEM = pl.BlockSpec(memory_space=pltpu.VMEM)
SMEM = pl.BlockSpec(memory_space=pltpu.SMEM)
ANY = pl.BlockSpec(memory_space=pl.ANY)


def pack_kernel(planes, place_ref, gate_ref, up_ref, down_ref, *rest):
    outs, sems = rest[:planes], rest[planes]
    plane = place_ref[0]
    copies = []
    for k in range(planes):
        owner = plane ^ k
        for w, ref in enumerate((gate_ref, up_ref, down_ref)):
            copies.append(pltpu.make_async_copy(ref.at[owner], outs[k].at[w], sems.at[3 * k + w]))
    for copy in copies:
        copy.start()
    for copy in copies:
        copy.wait()


def pack(place, gate, up, down):
    planes, rows, ff = gate.shape
    return pl.pallas_call(
        functools.partial(pack_kernel, planes),
        out_shape=[jax.ShapeDtypeStruct((3, rows, ff), gate.dtype)] * planes,
        in_specs=[SMEM, ANY, ANY, ANY],
        out_specs=[VMEM] * planes,
        scratch_shapes=[pltpu.SemaphoreType.DMA((3 * planes,))],
        name="pack_weights",
    )(place, gate, up, down)


def attend_kernel(blocks, live_ref, spot_ref, allowed_ref, query_in, target_ref, out_w_in, hidden_in, gain_ref, *rest):
    kv_in = rest[:blocks]
    attention_ref, residual_ref, outgoing_ref = rest[blocks : blocks + 3]
    query_ref, out_w_ref, hidden_ref, kv, packed, scores, top, total, acc, attended, sems = rest[blocks + 3 :]
    rows = query_ref.shape[0]
    chunk = scores.shape[2]
    tiles = live_ref.shape[0]
    per_chunk = chunk // TILE
    first = [pltpu.make_async_copy(query_in, query_ref, sems.at[0])]
    for i in range(blocks):
        first.append(pltpu.make_async_copy(kv_in[i], kv.at[pl.ds(i * rows, rows)], sems.at[3 + i]))
    late = [
        pltpu.make_async_copy(hidden_in, hidden_ref, sems.at[1]),
        pltpu.make_async_copy(out_w_in, out_w_ref, sems.at[2]),
    ]
    for copy in first + late:
        copy.start()
    for copy in first:
        copy.wait()

    @pl.loop(0, tiles)
    def _(i):
        @pl.when(live_ref[i] > 0)
        def _():
            source = pl.ds(pl.multiple_of(i * TILE, TILE), TILE)
            packed[pl.ds(pl.multiple_of(spot_ref[i] * TILE, TILE), TILE), :] = kv[source, :]

    used = spot_ref[tiles - 1] + live_ref[tiles - 1]
    chunks = (used + per_chunk - 1) // per_chunk

    @pl.loop(used, chunks * per_chunk)
    def _(i):
        packed[pl.ds(pl.multiple_of(i * TILE, TILE), TILE), :] = jnp.zeros((TILE, 2 * KVW), jnp.bfloat16)

    lane_tile = lax.broadcasted_iota(jnp.int32, (128, chunk), 1) // TILE
    widen = (lane_tile == lax.broadcasted_iota(jnp.int32, (128, chunk), 0)).astype(jnp.float32).astype(jnp.bfloat16)
    scale = HEAD ** (-0.5)
    for h in range(KV_HEADS):
        heads = [query_ref[:, (h * GROUPS + g) * HEAD : (h * GROUPS + g + 1) * HEAD] for g in range(GROUPS)]
        query = jnp.concatenate(heads, axis=0)
        top[...] = jnp.full(top.shape, -1e30, jnp.float32)
        total[...] = jnp.zeros(total.shape, jnp.float32)
        acc[...] = jnp.zeros(acc.shape, jnp.float32)

        @pl.loop(0, chunks)
        def _(j):
            keys = packed[pl.ds(pl.multiple_of(j * chunk, 128), chunk), h * HEAD : (h + 1) * HEAD]
            s = lax.dot_general(query, keys, (((1,), (1,)), ((), ())), preferred_element_type=jnp.float32)
            allowed = jnp.dot(allowed_ref[j], widen, preferred_element_type=jnp.float32)
            bias = (allowed - 1.0) * 1e30
            bias = [jnp.broadcast_to(bias[t : t + 1], (TILE, chunk)) for t in range(rows // TILE)]
            bias = jnp.concatenate(bias, axis=0)
            s = s.reshape(GROUPS, rows, chunk) + bias[None]
            s = s.reshape(GROUPS * rows, chunk)
            scores[j] = s
            best = top[...]
            for c in range(0, chunk, 128):
                best = jnp.maximum(best, s[:, c : c + 128])
            top[...] = best

        highest = jnp.max(top[...], axis=1, keepdims=True)
        top[...] = jnp.broadcast_to(highest, top.shape)

        @pl.loop(0, chunks)
        def _(j):
            values = packed[pl.ds(pl.multiple_of(j * chunk, 128), chunk), KVW + h * HEAD : KVW + (h + 1) * HEAD]
            high = top[...]
            s = scores[j]
            parts = []
            running = total[...]
            for c in range(0, chunk, 128):
                w = jnp.exp((s[:, c : c + 128] - high) * scale)
                running = running + w
                parts.append(w.astype(jnp.bfloat16))
            total[...] = running
            weights = jnp.concatenate(parts, axis=1)
            acc[...] += jnp.dot(weights, values, preferred_element_type=jnp.float32)

        denominator = jnp.sum(total[...], axis=1, keepdims=True)
        result = (acc[...] / denominator).astype(jnp.bfloat16)
        for g in range(GROUPS):
            col = (h * GROUPS + g) * HEAD
            attended[:, col : col + HEAD] = result[g * rows : (g + 1) * rows]
    for copy in late:
        copy.wait()
    projected = jnp.dot(attended[...], out_w_ref[...], preferred_element_type=jnp.float32)
    attention_ref[...] = projected.astype(jnp.bfloat16)
    residual = (hidden_ref[...].astype(jnp.float32) + projected).astype(jnp.bfloat16)
    residual_ref[...] = residual
    wide = residual.astype(jnp.float32)
    inverse = lax.rsqrt(jnp.mean(wide * wide, axis=-1, keepdims=True) + 1e-05)
    normed = (wide * inverse * gain_ref[...]).astype(jnp.bfloat16)
    slot = lax.broadcasted_iota(jnp.int32, (SLOTS, rows), 0)
    chosen = (slot == target_ref[0:1, :]) | (slot == target_ref[1:2, :])
    selector = chosen.astype(jnp.float32).astype(jnp.bfloat16)
    outgoing_ref[...] = jnp.dot(selector, normed, preferred_element_type=jnp.float32).astype(jnp.bfloat16)


def attend(live, spot, allowed, query, target, out_w, hidden, gain, blocks):
    rows = query.shape[0]
    chunks = allowed.shape[0]
    n = len(blocks)
    chunk = n * rows // chunks
    return pl.pallas_call(
        functools.partial(attend_kernel, n),
        out_shape=[
            jax.ShapeDtypeStruct((rows, D), jnp.bfloat16),
            jax.ShapeDtypeStruct((rows, D), jnp.bfloat16),
            jax.ShapeDtypeStruct((SLOTS, D), jnp.bfloat16),
        ],
        in_specs=[SMEM, SMEM, VMEM, ANY, VMEM, ANY, ANY, VMEM] + [ANY] * n,
        out_specs=[VMEM] * 3,
        scratch_shapes=[
            pltpu.VMEM((rows, D), jnp.bfloat16),
            pltpu.VMEM((D, D), jnp.bfloat16),
            pltpu.VMEM((rows, D), jnp.bfloat16),
            pltpu.VMEM((n * rows, 2 * KVW), jnp.bfloat16),
            pltpu.VMEM((n * rows, 2 * KVW), jnp.bfloat16),
            pltpu.VMEM((chunks, GROUPS * rows, chunk), jnp.float32),
            pltpu.VMEM((GROUPS * rows, HEAD), jnp.float32),
            pltpu.VMEM((GROUPS * rows, HEAD), jnp.float32),
            pltpu.VMEM((GROUPS * rows, HEAD), jnp.float32),
            pltpu.VMEM((rows, D), jnp.bfloat16),
            pltpu.SemaphoreType.DMA((3 + n,)),
        ],
        compiler_params=pltpu.CompilerParams(vmem_limit_bytes=56 * MB),
        name="attend",
    )(live, spot, allowed, query, target, out_w, hidden, gain, *blocks)


def key_order(tile_mask, me, world):
    tiles, count = tile_mask.shape
    order = me ^ jnp.arange(world)
    mask = jnp.take(tile_mask.reshape(tiles, world, tiles), order, axis=1, mode="clip").reshape(tiles, count)
    mask = (mask > 0).astype(jnp.bfloat16)
    live = jnp.max(mask, axis=0)
    index = jnp.arange(count)
    spot = jnp.dot(live, (index[:, None] < index[None, :]).astype(jnp.bfloat16), preferred_element_type=jnp.float32)
    move = (spot[:, None] == index[None, :].astype(jnp.float32)) & (live[:, None] > 0)
    placed = jnp.dot(mask, move.astype(jnp.bfloat16), preferred_element_type=jnp.float32)
    per_chunk = 2 * tiles
    placed = placed.reshape(tiles, count // per_chunk, per_chunk).transpose(1, 0, 2)
    placed = jnp.pad(placed, ((0, 0), (0, -tiles % 16), (0, 128 - per_chunk))).astype(jnp.bfloat16)
    return live.astype(jnp.int32), spot.astype(jnp.int32), placed


def expert_kernel(planes, shared, place_ref, rows_ref, *rest):
    count = planes * shared
    pieces = rest[:count]
    out_ref, gate, up, down, total, sems = rest[count:]
    depth, ff = pieces[0].shape[1:]
    plane, seat = place_ref[0], place_ref[1]
    copies = [[], [], []]
    for w, full in enumerate((gate, up, down)):
        for m in range(shared):
            for k in range(planes):
                at = ((plane ^ k) * shared + (seat ^ m)) * depth
                target = full.at[pl.ds(pl.multiple_of(at, depth), depth), :]
                n = m * planes + k
                copies[w].append(pltpu.make_async_copy(pieces[n].at[w], target, sems.at[w * count + n]))
    for group in copies:
        for copy in group:
            copy.start()
    for group in copies[:2]:
        for copy in group:
            copy.wait()
    step = 256
    for n, c in enumerate(range(0, ff, step)):
        rows = rows_ref[...]
        gated = jnp.dot(rows, gate[:, c : c + step], preferred_element_type=jnp.float32)
        upper = jnp.dot(rows, up[:, c : c + step], preferred_element_type=jnp.float32)
        hidden = (gated / (1.0 + jnp.exp(-gated)) * upper).astype(jnp.bfloat16)
        if n == 0:
            for copy in copies[2]:
                copy.wait()
        part = lax.dot_general(
            hidden, down[:, c : c + step], (((1,), (1,)), ((), ())), preferred_element_type=jnp.float32
        )
        if n == 0:
            total[...] = part
        else:
            total[...] += part
    out_ref[...] = total[...].astype(jnp.bfloat16)


def run_expert(place, rows, pieces, planes, shared):
    depth, ff = pieces[0].shape[1:]
    count = planes * shared
    return pl.pallas_call(
        functools.partial(expert_kernel, planes, shared),
        out_shape=jax.ShapeDtypeStruct(rows.shape, jnp.bfloat16),
        in_specs=[SMEM, VMEM] + [ANY] * count,
        out_specs=VMEM,
        scratch_shapes=[
            pltpu.VMEM((D, ff), jnp.bfloat16),
            pltpu.VMEM((D, ff), jnp.bfloat16),
            pltpu.VMEM((D, ff), jnp.bfloat16),
            pltpu.VMEM(rows.shape, jnp.float32),
            pltpu.SemaphoreType.DMA((3 * count,)),
        ],
        compiler_params=pltpu.CompilerParams(vmem_limit_bytes=60 * MB),
        name="expert",
    )(place, rows, *pieces)


def combine_kernel(returned_ref, target_ref, probs_ref, residual_ref, out_ref):
    rows = residual_ref.shape[0]
    slot = lax.broadcasted_iota(jnp.int32, (rows, SLOTS), 1)
    returned = returned_ref[...]
    total = jnp.zeros((rows, D), jnp.float32)
    for k in range(TOP):
        selector = (slot == target_ref[:, k : k + 1]).astype(jnp.float32).astype(jnp.bfloat16)
        picked = jnp.dot(selector, returned, preferred_element_type=jnp.float32)
        total = total + picked * probs_ref[:, k : k + 1]
    out_ref[...] = (residual_ref[...].astype(jnp.float32) + total).astype(jnp.bfloat16)


def combine(returned, target, probs, residual):
    return pl.pallas_call(
        combine_kernel,
        out_shape=jax.ShapeDtypeStruct(residual.shape, jnp.bfloat16),
        in_specs=[VMEM] * 4,
        out_specs=VMEM,
        compiler_params=pltpu.CompilerParams(vmem_limit_bytes=16 * MB),
        name="combine",
    )(returned, target, probs, residual)


def slots_of(ids):
    rows = ids.shape[0]
    onehot = (ids[:, :, None] == jnp.arange(EXPERTS, dtype=jnp.int32)).astype(jnp.float32)
    named = jnp.sum(onehot, axis=1)
    earlier = (jnp.arange(rows)[:, None] > jnp.arange(rows)[None, :]).astype(jnp.bfloat16)
    before = jnp.dot(earlier, named.astype(jnp.bfloat16), preferred_element_type=jnp.float32)
    slot = jnp.sum(onehot * before[:, None, :], axis=2).astype(jnp.int32)
    return ids * CAP + slot


def shards(
    planes,
    shared,
    hidden_in,
    queries,
    key_proj,
    value_proj,
    tile_mask,
    out_weight,
    moe_gain,
    gate_weight,
    up_weight,
    down_weight,
    expert_ids,
    gate_probs,
):
    ctx = ("plane", "seat")
    world = planes * shared
    plane = lax.axis_index("plane")
    seat = lax.axis_index("seat")
    me = plane * shared + seat
    place = jnp.stack([plane, seat]).astype(jnp.int32)

    def swap(x, bit):
        return lax.ppermute(x, ctx, [(i, i ^ bit) for i in range(world)])

    blocks = {0: jnp.concatenate([key_proj[0], value_proj[0]], axis=1)}
    packed = pack(place, gate_weight, up_weight, down_weight)
    pieces = {(0, 0): packed[0]}
    bit = world // 2
    blocks[bit] = swap(blocks[0], bit)
    far = [k for k in range(planes) if k >= planes // 2 and k]
    near = [k for k in range(planes) if k < planes // 2 and k]
    if far:
        pieces[0, far[0]] = swap(packed[far[0]], far[0] * shared)
    for k in near:
        pieces[0, k] = swap(packed[k], k * shared)
    bit //= 2
    while bit:
        blocks.update({m | bit: swap(x, bit) for m, x in list(blocks.items())})
        bit //= 2
    if far:
        blocks, pieces[0, far[0]] = lax.optimization_barrier((blocks, pieces[0, far[0]]))
        last, pieces[0, far[0]] = lax.optimization_barrier((packed[far[1]], pieces[0, far[0]]))
        pieces[0, far[1]] = swap(last, far[1] * shared)
    bit = shared // 2
    while bit:
        pieces.update({(m | bit, k): swap(x, bit) for (m, k), x in list(pieces.items())})
        bit //= 2

    target = slots_of(expert_ids[0])
    live, spot, allowed = key_order(tile_mask[0], me, world)
    attention_out, residual, outgoing = attend(
        live,
        spot,
        allowed,
        queries[0],
        target.T,
        out_weight,
        hidden_in[0],
        moe_gain[None],
        [blocks[m] for m in range(world)],
    )
    arrived = lax.all_to_all(
        outgoing.reshape(EXPERTS, CAP, D), ("exp", "plane"), split_axis=0, concat_axis=0, tiled=True
    )
    expert_rows = run_expert(
        place,
        arrived.reshape(SLOTS, D),
        [pieces[m, k] for m in range(shared) for k in range(planes)],
        planes,
        shared,
    )
    returned = lax.all_to_all(
        expert_rows.reshape(EXPERTS, CAP, D), ("exp", "plane"), split_axis=0, concat_axis=0, tiled=True
    )
    layer_out = combine(returned.reshape(SLOTS, D), target, gate_probs[0], residual)
    return attention_out[None], layer_out[None]


def solution(mesh):
    n_ctx, n_exp = mesh.shape["ctx"], mesh.shape["exp"]
    planes = EXPERTS // n_exp
    shared = n_ctx // planes
    fine = Mesh(mesh.devices.reshape(planes, shared, n_exp), ("plane", "seat", "exp"))
    split = P("exp", ("plane", "seat"), None)
    return jax.shard_map(
        functools.partial(shards, planes, shared),
        mesh=fine,
        in_specs=(split, split, split, split, split, P(), P(), split, split, split, split, split),
        out_specs=(split, split),
        check_vma=False,
    )
```

```python
import functools

import jax
import jax.numpy as jnp
from jax import lax
from jax.experimental import pallas as pl
from jax.experimental.pallas import tpu as pltpu
from jax.sharding import Mesh, PartitionSpec as P

D = 1024
HEADS = 8
KV_HEADS = 2
EXPERTS = 8
TOP = 2
TILE = 32
CAP = 72
HEAD = D // HEADS
GROUPS = HEADS // KV_HEADS
KVW = KV_HEADS * HEAD
SLOTS = EXPERTS * CAP
MB = 1 << 20

VMEM = pl.BlockSpec(memory_space=pltpu.VMEM)
SMEM = pl.BlockSpec(memory_space=pltpu.SMEM)
ANY = pl.BlockSpec(memory_space=pl.ANY)


def pack_kernel(planes, place_ref, gate_ref, up_ref, down_ref, *rest):
    outs, sems = rest[:planes], rest[planes]
    plane = place_ref[0]
    copies = []
    for k in range(planes):
        owner = plane ^ k
        for w, ref in enumerate((gate_ref, up_ref, down_ref)):
            copies.append(pltpu.make_async_copy(ref.at[owner], outs[k].at[w], sems.at[3 * k + w]))
    for copy in copies:
        copy.start()
    for copy in copies:
        copy.wait()


def pack(place, gate, up, down):
    planes, rows, ff = gate.shape
    return pl.pallas_call(
        functools.partial(pack_kernel, planes),
        out_shape=[jax.ShapeDtypeStruct((3, rows, ff), gate.dtype)] * planes,
        in_specs=[SMEM, ANY, ANY, ANY],
        out_specs=[VMEM] * planes,
        scratch_shapes=[pltpu.SemaphoreType.DMA((3 * planes,))],
        name="pack_weights",
    )(place, gate, up, down)


def attend_kernel(blocks, live_ref, spot_ref, allowed_ref, query_in, target_ref, out_w_in, hidden_in, gain_ref, *rest):
    kv_in = rest[:blocks]
    attention_ref, residual_ref, outgoing_ref = rest[blocks : blocks + 3]
    query_ref, out_w_ref, hidden_ref, kv, packed, scores, top, total, acc, attended, sems = rest[blocks + 3 :]
    rows = query_ref.shape[0]
    chunk = scores.shape[2]
    tiles = live_ref.shape[0]
    per_chunk = chunk // TILE
    first = [pltpu.make_async_copy(query_in, query_ref, sems.at[0])]
    for i in range(blocks):
        first.append(pltpu.make_async_copy(kv_in[i], kv.at[pl.ds(i * rows, rows)], sems.at[3 + i]))
    late = [
        pltpu.make_async_copy(hidden_in, hidden_ref, sems.at[1]),
        pltpu.make_async_copy(out_w_in, out_w_ref, sems.at[2]),
    ]
    for copy in first + late:
        copy.start()
    for copy in first:
        copy.wait()

    @pl.loop(0, tiles)
    def _(i):
        @pl.when(live_ref[i] > 0)
        def _():
            source = pl.ds(pl.multiple_of(i * TILE, TILE), TILE)
            packed[pl.ds(pl.multiple_of(spot_ref[i] * TILE, TILE), TILE), :] = kv[source, :]

    used = spot_ref[tiles - 1] + live_ref[tiles - 1]
    chunks = (used + per_chunk - 1) // per_chunk

    @pl.loop(used, chunks * per_chunk)
    def _(i):
        packed[pl.ds(pl.multiple_of(i * TILE, TILE), TILE), :] = jnp.zeros((TILE, 2 * KVW), jnp.bfloat16)

    lane_tile = lax.broadcasted_iota(jnp.int32, (128, chunk), 1) // TILE
    widen = (lane_tile == lax.broadcasted_iota(jnp.int32, (128, chunk), 0)).astype(jnp.float32).astype(jnp.bfloat16)
    scale = HEAD ** (-0.5)
    for h in range(KV_HEADS):
        heads = [query_ref[:, (h * GROUPS + g) * HEAD : (h * GROUPS + g + 1) * HEAD] for g in range(GROUPS)]
        query = jnp.concatenate(heads, axis=0)
        top[...] = jnp.full(top.shape, -1e30, jnp.float32)
        total[...] = jnp.zeros(total.shape, jnp.float32)
        acc[...] = jnp.zeros(acc.shape, jnp.float32)

        @pl.loop(0, chunks)
        def _(j):
            keys = packed[pl.ds(pl.multiple_of(j * chunk, 128), chunk), h * HEAD : (h + 1) * HEAD]
            s = lax.dot_general(query, keys, (((1,), (1,)), ((), ())), preferred_element_type=jnp.float32)
            allowed = jnp.dot(allowed_ref[j], widen, preferred_element_type=jnp.float32)
            bias = (allowed - 1.0) * 1e30
            bias = [jnp.broadcast_to(bias[t : t + 1], (TILE, chunk)) for t in range(rows // TILE)]
            bias = jnp.concatenate(bias, axis=0)
            s = s.reshape(GROUPS, rows, chunk) + bias[None]
            s = s.reshape(GROUPS * rows, chunk)
            scores[j] = s
            best = top[...]
            for c in range(0, chunk, 128):
                best = jnp.maximum(best, s[:, c : c + 128])
            top[...] = best

        highest = jnp.max(top[...], axis=1, keepdims=True)
        top[...] = jnp.broadcast_to(highest, top.shape)

        @pl.loop(0, chunks)
        def _(j):
            values = packed[pl.ds(pl.multiple_of(j * chunk, 128), chunk), KVW + h * HEAD : KVW + (h + 1) * HEAD]
            high = top[...]
            s = scores[j]
            parts = []
            running = total[...]
            for c in range(0, chunk, 128):
                w = jnp.exp((s[:, c : c + 128] - high) * scale)
                running = running + w
                parts.append(w.astype(jnp.bfloat16))
            total[...] = running
            weights = jnp.concatenate(parts, axis=1)
            acc[...] += jnp.dot(weights, values, preferred_element_type=jnp.float32)

        denominator = jnp.sum(total[...], axis=1, keepdims=True)
        result = (acc[...] / denominator).astype(jnp.bfloat16)
        for g in range(GROUPS):
            col = (h * GROUPS + g) * HEAD
            attended[:, col : col + HEAD] = result[g * rows : (g + 1) * rows]
    for copy in late:
        copy.wait()
    projected = jnp.dot(attended[...], out_w_ref[...], preferred_element_type=jnp.float32)
    attention_ref[...] = projected.astype(jnp.bfloat16)
    residual = (hidden_ref[...].astype(jnp.float32) + projected).astype(jnp.bfloat16)
    residual_ref[...] = residual
    wide = residual.astype(jnp.float32)
    inverse = lax.rsqrt(jnp.mean(wide * wide, axis=-1, keepdims=True) + 1e-05)
    normed = (wide * inverse * gain_ref[...]).astype(jnp.bfloat16)
    slot = lax.broadcasted_iota(jnp.int32, (SLOTS, rows), 0)
    chosen = (slot == target_ref[0:1, :]) | (slot == target_ref[1:2, :])
    selector = chosen.astype(jnp.float32).astype(jnp.bfloat16)
    outgoing_ref[...] = jnp.dot(selector, normed, preferred_element_type=jnp.float32).astype(jnp.bfloat16)


def attend(live, spot, allowed, query, target, out_w, hidden, gain, blocks):
    rows = query.shape[0]
    chunks = allowed.shape[0]
    n = len(blocks)
    chunk = n * rows // chunks
    return pl.pallas_call(
        functools.partial(attend_kernel, n),
        out_shape=[
            jax.ShapeDtypeStruct((rows, D), jnp.bfloat16),
            jax.ShapeDtypeStruct((rows, D), jnp.bfloat16),
            jax.ShapeDtypeStruct((SLOTS, D), jnp.bfloat16),
        ],
        in_specs=[SMEM, SMEM, VMEM, ANY, VMEM, ANY, ANY, VMEM] + [ANY] * n,
        out_specs=[VMEM] * 3,
        scratch_shapes=[
            pltpu.VMEM((rows, D), jnp.bfloat16),
            pltpu.VMEM((D, D), jnp.bfloat16),
            pltpu.VMEM((rows, D), jnp.bfloat16),
            pltpu.VMEM((n * rows, 2 * KVW), jnp.bfloat16),
            pltpu.VMEM((n * rows, 2 * KVW), jnp.bfloat16),
            pltpu.VMEM((chunks, GROUPS * rows, chunk), jnp.float32),
            pltpu.VMEM((GROUPS * rows, HEAD), jnp.float32),
            pltpu.VMEM((GROUPS * rows, HEAD), jnp.float32),
            pltpu.VMEM((GROUPS * rows, HEAD), jnp.float32),
            pltpu.VMEM((rows, D), jnp.bfloat16),
            pltpu.SemaphoreType.DMA((3 + n,)),
        ],
        compiler_params=pltpu.CompilerParams(vmem_limit_bytes=56 * MB),
        name="attend",
    )(live, spot, allowed, query, target, out_w, hidden, gain, *blocks)


def key_order(tile_mask, me, world):
    tiles, count = tile_mask.shape
    order = me ^ jnp.arange(world)
    mask = jnp.take(tile_mask.reshape(tiles, world, tiles), order, axis=1, mode="clip").reshape(tiles, count)
    mask = (mask > 0).astype(jnp.bfloat16)
    live = jnp.max(mask, axis=0)
    index = jnp.arange(count)
    spot = jnp.dot(live, (index[:, None] < index[None, :]).astype(jnp.bfloat16), preferred_element_type=jnp.float32)
    move = (spot[:, None] == index[None, :].astype(jnp.float32)) & (live[:, None] > 0)
    placed = jnp.dot(mask, move.astype(jnp.bfloat16), preferred_element_type=jnp.float32)
    per_chunk = 2 * tiles
    placed = placed.reshape(tiles, count // per_chunk, per_chunk).transpose(1, 0, 2)
    placed = jnp.pad(placed, ((0, 0), (0, -tiles % 16), (0, 128 - per_chunk))).astype(jnp.bfloat16)
    return live.astype(jnp.int32), spot.astype(jnp.int32), placed


def expert_kernel(planes, shared, place_ref, rows_ref, *rest):
    count = planes * shared
    pieces = rest[:count]
    out_ref, gate, up, down, total, sems = rest[count:]
    depth, ff = pieces[0].shape[1:]
    plane, seat = place_ref[0], place_ref[1]
    copies = [[], [], []]
    for w, full in enumerate((gate, up, down)):
        for m in range(shared):
            for k in range(planes):
                at = ((plane ^ k) * shared + (seat ^ m)) * depth
                target = full.at[pl.ds(pl.multiple_of(at, depth), depth), :]
                n = m * planes + k
                copies[w].append(pltpu.make_async_copy(pieces[n].at[w], target, sems.at[w * count + n]))
    for group in copies:
        for copy in group:
            copy.start()
    for group in copies[:2]:
        for copy in group:
            copy.wait()
    step = 256
    for n, c in enumerate(range(0, ff, step)):
        rows = rows_ref[...]
        gated = jnp.dot(rows, gate[:, c : c + step], preferred_element_type=jnp.float32)
        upper = jnp.dot(rows, up[:, c : c + step], preferred_element_type=jnp.float32)
        hidden = (gated / (1.0 + jnp.exp(-gated)) * upper).astype(jnp.bfloat16)
        if n == 0:
            for copy in copies[2]:
                copy.wait()
        part = lax.dot_general(
            hidden, down[:, c : c + step], (((1,), (1,)), ((), ())), preferred_element_type=jnp.float32
        )
        if n == 0:
            total[...] = part
        else:
            total[...] += part
    out_ref[...] = total[...].astype(jnp.bfloat16)


def run_expert(place, rows, pieces, planes, shared):
    depth, ff = pieces[0].shape[1:]
    count = planes * shared
    return pl.pallas_call(
        functools.partial(expert_kernel, planes, shared),
        out_shape=jax.ShapeDtypeStruct(rows.shape, jnp.bfloat16),
        in_specs=[SMEM, VMEM] + [ANY] * count,
        out_specs=VMEM,
        scratch_shapes=[
            pltpu.VMEM((D, ff), jnp.bfloat16),
            pltpu.VMEM((D, ff), jnp.bfloat16),
            pltpu.VMEM((D, ff), jnp.bfloat16),
            pltpu.VMEM(rows.shape, jnp.float32),
            pltpu.SemaphoreType.DMA((3 * count,)),
        ],
        compiler_params=pltpu.CompilerParams(vmem_limit_bytes=60 * MB),
        name="expert",
    )(place, rows, *pieces)


def combine_kernel(returned_ref, target_ref, probs_ref, residual_ref, out_ref):
    rows = residual_ref.shape[0]
    slot = lax.broadcasted_iota(jnp.int32, (rows, SLOTS), 1)
    returned = returned_ref[...]
    total = jnp.zeros((rows, D), jnp.float32)
    for k in range(TOP):
        selector = (slot == target_ref[:, k : k + 1]).astype(jnp.float32).astype(jnp.bfloat16)
        picked = jnp.dot(selector, returned, preferred_element_type=jnp.float32)
        total = total + picked * probs_ref[:, k : k + 1]
    out_ref[...] = (residual_ref[...].astype(jnp.float32) + total).astype(jnp.bfloat16)


def combine(returned, target, probs, residual):
    return pl.pallas_call(
        combine_kernel,
        out_shape=jax.ShapeDtypeStruct(residual.shape, jnp.bfloat16),
        in_specs=[VMEM] * 4,
        out_specs=VMEM,
        compiler_params=pltpu.CompilerParams(vmem_limit_bytes=16 * MB),
        name="combine",
    )(returned, target, probs, residual)


def slots_of(ids):
    rows = ids.shape[0]
    onehot = (ids[:, :, None] == jnp.arange(EXPERTS, dtype=jnp.int32)).astype(jnp.float32)
    named = jnp.sum(onehot, axis=1)
    earlier = (jnp.arange(rows)[:, None] > jnp.arange(rows)[None, :]).astype(jnp.bfloat16)
    before = jnp.dot(earlier, named.astype(jnp.bfloat16), preferred_element_type=jnp.float32)
    slot = jnp.sum(onehot * before[:, None, :], axis=2).astype(jnp.int32)
    return ids * CAP + slot


def shards(
    planes,
    shared,
    hidden_in,
    queries,
    key_proj,
    value_proj,
    tile_mask,
    out_weight,
    moe_gain,
    gate_weight,
    up_weight,
    down_weight,
    expert_ids,
    gate_probs,
):
    ctx = ("plane", "seat")
    world = planes * shared
    plane = lax.axis_index("plane")
    seat = lax.axis_index("seat")
    me = plane * shared + seat
    place = jnp.stack([plane, seat]).astype(jnp.int32)

    def swap(x, bit):
        return lax.ppermute(x, ctx, [(i, i ^ bit) for i in range(world)])

    def tie(value, places):
        places = [at for at in places if at in pieces]
        value, found = lax.optimization_barrier((value, [pieces[at] for at in places]))
        pieces.update(zip(places, found))
        return value

    target = slots_of(expert_ids[0])
    order = key_order(tile_mask[0], me, world)
    own = jnp.concatenate([key_proj[0], value_proj[0]], axis=1)
    bit = world // 2
    half = shared // 2
    blocks = {0: own, bit: swap(own, bit)}
    packed = pack(place, gate_weight, up_weight, down_weight)
    far = [k for k in range(planes) if k >= planes // 2 and k]
    near = [k for k in range(planes) if k < planes // 2 and k]
    pieces = {(0, 0): packed[0]}
    for k in far[:1] + near:
        pieces[0, k] = swap(packed[k], k * shared)
    pieces[half, 0] = swap(packed[0], half)
    bit //= 2
    while bit:
        if bit == 1:
            last = world - 2
            blocks[last] = tie(blocks[last], [(2, 0)])
            blocks[last], order, target = lax.optimization_barrier((blocks[last], order, target))
        blocks.update({m | bit: swap(x, bit) for m, x in list(blocks.items())})
        bit //= 2
    blocks = tie(blocks, [(0, 2)])
    if far:
        last = tie(packed[far[1]], [(0, far[0])])
        pieces[0, far[1]] = swap(last, far[1] * shared)
    bit = half
    while bit:
        for (m, k), x in list(pieces.items()):
            if (m | bit, k) not in pieces:
                pieces[m | bit, k] = swap(x, bit)
        bit //= 2

    live, spot, allowed = order
    attention_out, residual, outgoing = attend(
        live,
        spot,
        allowed,
        queries[0],
        target.T,
        out_weight,
        hidden_in[0],
        moe_gain[None],
        [blocks[m] for m in range(world)],
    )
    outgoing = tie(outgoing, [(2, 2)])
    arrived = lax.all_to_all(
        outgoing.reshape(EXPERTS, CAP, D), ("exp", "plane"), split_axis=0, concat_axis=0, tiled=True
    )
    expert_rows = run_expert(
        place,
        arrived.reshape(SLOTS, D),
        [pieces[m, k] for m in range(shared) for k in range(planes)],
        planes,
        shared,
    )
    returned = lax.all_to_all(
        expert_rows.reshape(EXPERTS, CAP, D), ("exp", "plane"), split_axis=0, concat_axis=0, tiled=True
    )
    layer_out = combine(returned.reshape(SLOTS, D), target, gate_probs[0], residual)
    return attention_out[None], layer_out[None]


def solution(mesh):
    n_ctx, n_exp = mesh.shape["ctx"], mesh.shape["exp"]
    planes = EXPERTS // n_exp
    shared = n_ctx // planes
    fine = Mesh(mesh.devices.reshape(planes, shared, n_exp), ("plane", "seat", "exp"))
    split = P("exp", ("plane", "seat"), None)
    return jax.shard_map(
        functools.partial(shards, planes, shared),
        mesh=fine,
        in_specs=(split, split, split, split, split, P(), P(), split, split, split, split, split),
        out_specs=(split, split),
        check_vma=False,
    )
```

```python
import functools

import jax
import jax.numpy as jnp
from jax import lax
from jax.experimental import pallas as pl
from jax.experimental.pallas import tpu as pltpu
from jax.sharding import Mesh, PartitionSpec as P

D = 1024
HEADS = 8
KV_HEADS = 2
EXPERTS = 8
TOP = 2
TILE = 32
CAP = 72
HEAD = D // HEADS
GROUPS = HEADS // KV_HEADS
KVW = KV_HEADS * HEAD
SLOTS = EXPERTS * CAP
MB = 1 << 20

VMEM = pl.BlockSpec(memory_space=pltpu.VMEM)
SMEM = pl.BlockSpec(memory_space=pltpu.SMEM)
ANY = pl.BlockSpec(memory_space=pl.ANY)


def pack_kernel(planes, place_ref, gate_ref, up_ref, down_ref, *rest):
    outs, sems = rest[:planes], rest[planes]
    plane = place_ref[0]
    copies = []
    for k in range(planes):
        owner = plane ^ k
        for w, ref in enumerate((gate_ref, up_ref, down_ref)):
            copies.append(pltpu.make_async_copy(ref.at[owner], outs[k].at[w], sems.at[3 * k + w]))
    for copy in copies:
        copy.start()
    for copy in copies:
        copy.wait()


def pack(place, gate, up, down):
    planes, rows, ff = gate.shape
    return pl.pallas_call(
        functools.partial(pack_kernel, planes),
        out_shape=[jax.ShapeDtypeStruct((3, rows, ff), gate.dtype)] * planes,
        in_specs=[SMEM, ANY, ANY, ANY],
        out_specs=[VMEM] * planes,
        scratch_shapes=[pltpu.SemaphoreType.DMA((3 * planes,))],
        name="pack_weights",
    )(place, gate, up, down)


def attend_kernel(blocks, live_ref, spot_ref, allowed_ref, query_in, target_ref, out_w_in, hidden_in, gain_ref, *rest):
    kv_in = rest[:blocks]
    attention_ref, residual_ref, outgoing_ref = rest[blocks : blocks + 3]
    query_ref, out_w_ref, hidden_ref, kv, packed, scores, top, total, acc, attended, sems = rest[blocks + 3 :]
    rows = query_ref.shape[0]
    chunk = scores.shape[2]
    tiles = live_ref.shape[0]
    per_chunk = chunk // TILE
    first = [pltpu.make_async_copy(query_in, query_ref, sems.at[0])]
    for i in range(blocks):
        first.append(pltpu.make_async_copy(kv_in[i], kv.at[pl.ds(i * rows, rows)], sems.at[3 + i]))
    late = [
        pltpu.make_async_copy(hidden_in, hidden_ref, sems.at[1]),
        pltpu.make_async_copy(out_w_in, out_w_ref, sems.at[2]),
    ]
    for copy in first + late:
        copy.start()
    for copy in first:
        copy.wait()

    @pl.loop(0, tiles)
    def _(i):
        @pl.when(live_ref[i] > 0)
        def _():
            source = pl.ds(pl.multiple_of(i * TILE, TILE), TILE)
            packed[pl.ds(pl.multiple_of(spot_ref[i] * TILE, TILE), TILE), :] = kv[source, :]

    used = spot_ref[tiles - 1] + live_ref[tiles - 1]
    chunks = (used + per_chunk - 1) // per_chunk

    @pl.loop(used, chunks * per_chunk)
    def _(i):
        packed[pl.ds(pl.multiple_of(i * TILE, TILE), TILE), :] = jnp.zeros((TILE, 2 * KVW), jnp.bfloat16)

    lane_tile = lax.broadcasted_iota(jnp.int32, (128, chunk), 1) // TILE
    widen = (lane_tile == lax.broadcasted_iota(jnp.int32, (128, chunk), 0)).astype(jnp.float32).astype(jnp.bfloat16)
    scale = HEAD ** (-0.5)
    for h in range(KV_HEADS):
        heads = [query_ref[:, (h * GROUPS + g) * HEAD : (h * GROUPS + g + 1) * HEAD] for g in range(GROUPS)]
        query = jnp.concatenate(heads, axis=0)
        top[...] = jnp.full(top.shape, -1e30, jnp.float32)
        total[...] = jnp.zeros(total.shape, jnp.float32)
        acc[...] = jnp.zeros(acc.shape, jnp.float32)

        @pl.loop(0, chunks)
        def _(j):
            keys = packed[pl.ds(pl.multiple_of(j * chunk, 128), chunk), h * HEAD : (h + 1) * HEAD]
            s = lax.dot_general(query, keys, (((1,), (1,)), ((), ())), preferred_element_type=jnp.float32)
            allowed = jnp.dot(allowed_ref[j], widen, preferred_element_type=jnp.float32)
            bias = (allowed - 1.0) * 1e30
            bias = [jnp.broadcast_to(bias[t : t + 1], (TILE, chunk)) for t in range(rows // TILE)]
            bias = jnp.concatenate(bias, axis=0)
            s = s.reshape(GROUPS, rows, chunk) + bias[None]
            s = s.reshape(GROUPS * rows, chunk)
            scores[j] = s
            best = top[...]
            for c in range(0, chunk, 128):
                best = jnp.maximum(best, s[:, c : c + 128])
            top[...] = best

        highest = jnp.max(top[...], axis=1, keepdims=True)
        top[...] = jnp.broadcast_to(highest, top.shape)

        @pl.loop(0, chunks)
        def _(j):
            values = packed[pl.ds(pl.multiple_of(j * chunk, 128), chunk), KVW + h * HEAD : KVW + (h + 1) * HEAD]
            high = top[...]
            s = scores[j]
            parts = []
            running = total[...]
            for c in range(0, chunk, 128):
                w = jnp.exp((s[:, c : c + 128] - high) * scale)
                running = running + w
                parts.append(w.astype(jnp.bfloat16))
            total[...] = running
            weights = jnp.concatenate(parts, axis=1)
            acc[...] += jnp.dot(weights, values, preferred_element_type=jnp.float32)

        denominator = jnp.sum(total[...], axis=1, keepdims=True)
        result = (acc[...] / denominator).astype(jnp.bfloat16)
        for g in range(GROUPS):
            col = (h * GROUPS + g) * HEAD
            attended[:, col : col + HEAD] = result[g * rows : (g + 1) * rows]
    for copy in late:
        copy.wait()
    projected = jnp.dot(attended[...], out_w_ref[...], preferred_element_type=jnp.float32)
    attention_ref[...] = projected.astype(jnp.bfloat16)
    residual = (hidden_ref[...].astype(jnp.float32) + projected).astype(jnp.bfloat16)
    residual_ref[...] = residual
    wide = residual.astype(jnp.float32)
    inverse = lax.rsqrt(jnp.mean(wide * wide, axis=-1, keepdims=True) + 1e-05)
    normed = (wide * inverse * gain_ref[...]).astype(jnp.bfloat16)
    slot = lax.broadcasted_iota(jnp.int32, (SLOTS, rows), 0)
    chosen = (slot == target_ref[0:1, :]) | (slot == target_ref[1:2, :])
    selector = chosen.astype(jnp.float32).astype(jnp.bfloat16)
    outgoing_ref[...] = jnp.dot(selector, normed, preferred_element_type=jnp.float32).astype(jnp.bfloat16)


def attend(live, spot, allowed, query, target, out_w, hidden, gain, blocks):
    rows = query.shape[0]
    chunks = allowed.shape[0]
    n = len(blocks)
    chunk = n * rows // chunks
    return pl.pallas_call(
        functools.partial(attend_kernel, n),
        out_shape=[
            jax.ShapeDtypeStruct((rows, D), jnp.bfloat16),
            jax.ShapeDtypeStruct((rows, D), jnp.bfloat16),
            jax.ShapeDtypeStruct((SLOTS, D), jnp.bfloat16),
        ],
        in_specs=[SMEM, SMEM, VMEM, ANY, VMEM, ANY, ANY, VMEM] + [ANY] * n,
        out_specs=[VMEM] * 3,
        scratch_shapes=[
            pltpu.VMEM((rows, D), jnp.bfloat16),
            pltpu.VMEM((D, D), jnp.bfloat16),
            pltpu.VMEM((rows, D), jnp.bfloat16),
            pltpu.VMEM((n * rows, 2 * KVW), jnp.bfloat16),
            pltpu.VMEM((n * rows, 2 * KVW), jnp.bfloat16),
            pltpu.VMEM((chunks, GROUPS * rows, chunk), jnp.float32),
            pltpu.VMEM((GROUPS * rows, HEAD), jnp.float32),
            pltpu.VMEM((GROUPS * rows, HEAD), jnp.float32),
            pltpu.VMEM((GROUPS * rows, HEAD), jnp.float32),
            pltpu.VMEM((rows, D), jnp.bfloat16),
            pltpu.SemaphoreType.DMA((3 + n,)),
        ],
        compiler_params=pltpu.CompilerParams(vmem_limit_bytes=56 * MB),
        name="attend",
    )(live, spot, allowed, query, target, out_w, hidden, gain, *blocks)


def key_order(tile_mask, me, world):
    tiles, count = tile_mask.shape
    order = me ^ jnp.arange(world)
    mask = jnp.take(tile_mask.reshape(tiles, world, tiles), order, axis=1, mode="clip").reshape(tiles, count)
    mask = (mask > 0).astype(jnp.bfloat16)
    live = jnp.max(mask, axis=0)
    index = jnp.arange(count)
    spot = jnp.dot(live, (index[:, None] < index[None, :]).astype(jnp.bfloat16), preferred_element_type=jnp.float32)
    move = (spot[:, None] == index[None, :].astype(jnp.float32)) & (live[:, None] > 0)
    placed = jnp.dot(mask, move.astype(jnp.bfloat16), preferred_element_type=jnp.float32)
    per_chunk = 2 * tiles
    placed = placed.reshape(tiles, count // per_chunk, per_chunk).transpose(1, 0, 2)
    placed = jnp.pad(placed, ((0, 0), (0, -tiles % 16), (0, 128 - per_chunk))).astype(jnp.bfloat16)
    return live.astype(jnp.int32), spot.astype(jnp.int32), placed


def expert_kernel(planes, shared, cuts, step, place_ref, rows_in, *rest):
    count = planes * shared
    pieces = rest[:count]
    out_ref, rows_ref, full, total, sems = rest[count:]
    depth = pieces[0].shape[1]
    plane, seat = place_ref[0], place_ref[1]
    rows_copy = pltpu.make_async_copy(rows_in, rows_ref, sems.at[count * len(cuts)])
    copies = []
    for c, (low, high) in enumerate(cuts):
        for n in range(count):
            m, k = divmod(n, planes)
            at = ((plane ^ k) * shared + (seat ^ m)) * depth
            target = full.at[:, pl.ds(pl.multiple_of(at, depth), depth), pl.ds(low, high - low)]
            copies.append(pltpu.make_async_copy(pieces[n].at[:, :, pl.ds(low, high - low)], target, sems.at[c * count + n]))
            copies[-1].start()
        if c == 0:
            rows_copy.start()
    rows_copy.wait()
    for c, (low, high) in enumerate(cuts):
        for copy in copies[c * count : (c + 1) * count]:
            copy.wait()
        for at in range(low, high, step):
            rows = rows_ref[...]
            gated = jnp.dot(rows, full[0, :, at : at + step], preferred_element_type=jnp.float32)
            upper = jnp.dot(rows, full[1, :, at : at + step], preferred_element_type=jnp.float32)
            hidden = (gated / (1.0 + jnp.exp(-gated)) * upper).astype(jnp.bfloat16)
            part = lax.dot_general(
                hidden, full[2, :, at : at + step], (((1,), (1,)), ((), ())), preferred_element_type=jnp.float32
            )
            if at == 0:
                total[...] = part
            else:
                total[...] += part
    out_ref[...] = total[...].astype(jnp.bfloat16)


def run_expert(place, rows, pieces, planes, shared):
    depth, ff = pieces[0].shape[1:]
    count = planes * shared
    step = 256
    edges = [0, step, 3 * step, ff]
    cuts = list(zip(edges[:-1], edges[1:]))
    return pl.pallas_call(
        functools.partial(expert_kernel, planes, shared, cuts, step),
        out_shape=jax.ShapeDtypeStruct(rows.shape, jnp.bfloat16),
        in_specs=[SMEM, ANY] + [ANY] * count,
        out_specs=VMEM,
        scratch_shapes=[
            pltpu.VMEM(rows.shape, jnp.bfloat16),
            pltpu.VMEM((3, D, ff), jnp.bfloat16),
            pltpu.VMEM(rows.shape, jnp.float32),
            pltpu.SemaphoreType.DMA((count * len(cuts) + 1,)),
        ],
        compiler_params=pltpu.CompilerParams(vmem_limit_bytes=60 * MB),
        name="expert",
    )(place, rows, *pieces)


def combine_kernel(returned_ref, target_ref, probs_ref, residual_ref, out_ref):
    rows = residual_ref.shape[0]
    slot = lax.broadcasted_iota(jnp.int32, (rows, SLOTS), 1)
    returned = returned_ref[...]
    total = jnp.zeros((rows, D), jnp.float32)
    for k in range(TOP):
        selector = (slot == target_ref[:, k : k + 1]).astype(jnp.float32).astype(jnp.bfloat16)
        picked = jnp.dot(selector, returned, preferred_element_type=jnp.float32)
        total = total + picked * probs_ref[:, k : k + 1]
    out_ref[...] = (residual_ref[...].astype(jnp.float32) + total).astype(jnp.bfloat16)


def combine(returned, target, probs, residual):
    return pl.pallas_call(
        combine_kernel,
        out_shape=jax.ShapeDtypeStruct(residual.shape, jnp.bfloat16),
        in_specs=[VMEM] * 4,
        out_specs=VMEM,
        compiler_params=pltpu.CompilerParams(vmem_limit_bytes=16 * MB),
        name="combine",
    )(returned, target, probs, residual)


def slots_of(ids):
    rows = ids.shape[0]
    onehot = (ids[:, :, None] == jnp.arange(EXPERTS, dtype=jnp.int32)).astype(jnp.float32)
    named = jnp.sum(onehot, axis=1)
    earlier = (jnp.arange(rows)[:, None] > jnp.arange(rows)[None, :]).astype(jnp.bfloat16)
    before = jnp.dot(earlier, named.astype(jnp.bfloat16), preferred_element_type=jnp.float32)
    slot = jnp.sum(onehot * before[:, None, :], axis=2).astype(jnp.int32)
    return ids * CAP + slot


def shards(
    planes,
    shared,
    hidden_in,
    queries,
    key_proj,
    value_proj,
    tile_mask,
    out_weight,
    moe_gain,
    gate_weight,
    up_weight,
    down_weight,
    expert_ids,
    gate_probs,
):
    ctx = ("plane", "seat")
    world = planes * shared
    plane = lax.axis_index("plane")
    seat = lax.axis_index("seat")
    me = plane * shared + seat
    place = jnp.stack([plane, seat]).astype(jnp.int32)

    def swap(x, bit):
        return lax.ppermute(x, ctx, [(i, i ^ bit) for i in range(world)])

    def tie(value, places):
        places = [at for at in places if at in pieces]
        value, found = lax.optimization_barrier((value, [pieces[at] for at in places]))
        pieces.update(zip(places, found))
        return value

    target = slots_of(expert_ids[0])
    order = key_order(tile_mask[0], me, world)
    own = jnp.concatenate([key_proj[0], value_proj[0]], axis=1)
    bit = world // 2
    half = shared // 2
    blocks = {0: own, bit: swap(own, bit)}
    packed = pack(place, gate_weight, up_weight, down_weight)
    far = [k for k in range(planes) if k >= planes // 2 and k]
    near = [k for k in range(planes) if k < planes // 2 and k]
    pieces = {(0, 0): packed[0]}
    for k in far[:1] + near:
        pieces[0, k] = swap(packed[k], k * shared)
    pieces[half, 0] = swap(packed[0], half)
    bit //= 2
    while bit:
        if bit == 1:
            last = world - 2
            blocks[last] = tie(blocks[last], [(2, 0)])
            blocks[last], order, target = lax.optimization_barrier((blocks[last], order, target))
            if far:
                early = half + shared
                blocks[early], second = lax.optimization_barrier((blocks[early], packed[far[1]]))
                pieces[0, far[1]] = swap(second, far[1] * shared)
        blocks.update({m | bit: swap(x, bit) for m, x in list(blocks.items())})
        bit //= 2
    blocks = tie(blocks, [(0, 2)])
    bit = half
    while bit:
        for (m, k), x in list(pieces.items()):
            if (m | bit, k) not in pieces:
                pieces[m | bit, k] = swap(x, bit)
        bit //= 2

    live, spot, allowed = order
    attention_out, residual, outgoing = attend(
        live,
        spot,
        allowed,
        queries[0],
        target.T,
        out_weight,
        hidden_in[0],
        moe_gain[None],
        [blocks[m] for m in range(world)],
    )
    outgoing = tie(outgoing, [(2, 2)])
    arrived = lax.all_to_all(
        outgoing.reshape(EXPERTS, CAP, D), ("exp", "plane"), split_axis=0, concat_axis=0, tiled=True
    )
    expert_rows = run_expert(
        place,
        arrived.reshape(SLOTS, D),
        [pieces[m, k] for m in range(shared) for k in range(planes)],
        planes,
        shared,
    )
    returned = lax.all_to_all(
        expert_rows.reshape(EXPERTS, CAP, D), ("exp", "plane"), split_axis=0, concat_axis=0, tiled=True
    )
    layer_out = combine(returned.reshape(SLOTS, D), target, gate_probs[0], residual)
    return attention_out[None], layer_out[None]


def solution(mesh):
    n_ctx, n_exp = mesh.shape["ctx"], mesh.shape["exp"]
    planes = EXPERTS // n_exp
    shared = n_ctx // planes
    fine = Mesh(mesh.devices.reshape(planes, shared, n_exp), ("plane", "seat", "exp"))
    split = P("exp", ("plane", "seat"), None)
    return jax.shard_map(
        functools.partial(shards, planes, shared),
        mesh=fine,
        in_specs=(split, split, split, split, split, P(), P(), split, split, split, split, split),
        out_specs=(split, split),
        check_vma=False,
    )
```

```python
import functools

import jax
import jax.numpy as jnp
from jax import lax
from jax.experimental import pallas as pl
from jax.experimental.pallas import tpu as pltpu
from jax.sharding import Mesh, PartitionSpec as P

D = 1024
HEADS = 8
KV_HEADS = 2
EXPERTS = 8
TOP = 2
TILE = 32
CAP = 72
HEAD = D // HEADS
GROUPS = HEADS // KV_HEADS
KVW = KV_HEADS * HEAD
SLOTS = EXPERTS * CAP
MB = 1 << 20

VMEM = pl.BlockSpec(memory_space=pltpu.VMEM)
SMEM = pl.BlockSpec(memory_space=pltpu.SMEM)
ANY = pl.BlockSpec(memory_space=pl.ANY)


def pack_kernel(planes, place_ref, gate_ref, up_ref, down_ref, *rest):
    outs, sems = rest[:planes], rest[planes]
    plane = place_ref[0]
    copies = []
    for k in range(planes):
        owner = plane ^ k
        for w, ref in enumerate((gate_ref, up_ref, down_ref)):
            copies.append(pltpu.make_async_copy(ref.at[owner], outs[k].at[w], sems.at[3 * k + w]))
    for copy in copies:
        copy.start()
    for copy in copies:
        copy.wait()


def pack(place, gate, up, down):
    planes, rows, ff = gate.shape
    return pl.pallas_call(
        functools.partial(pack_kernel, planes),
        out_shape=[jax.ShapeDtypeStruct((3, rows, ff), gate.dtype)] * planes,
        in_specs=[SMEM, ANY, ANY, ANY],
        out_specs=[VMEM] * planes,
        scratch_shapes=[pltpu.SemaphoreType.DMA((3 * planes,))],
        name="pack_weights",
    )(place, gate, up, down)


def attend_kernel(blocks, live_ref, spot_ref, allowed_ref, query_in, target_ref, out_w_in, hidden_in, gain_ref, *rest):
    kv_in = rest[:blocks]
    attention_ref, residual_ref, outgoing_ref = rest[blocks : blocks + 3]
    query_ref, out_w_ref, hidden_ref, kv, packed, scores, top, total, acc, attended, sems = rest[blocks + 3 :]
    rows = query_ref.shape[0]
    chunk = scores.shape[2]
    tiles = live_ref.shape[0]
    per_chunk = chunk // TILE
    first = [pltpu.make_async_copy(query_in, query_ref, sems.at[0])]
    for i in range(blocks):
        first.append(pltpu.make_async_copy(kv_in[i], kv.at[pl.ds(i * rows, rows)], sems.at[3 + i]))
    late = [
        pltpu.make_async_copy(hidden_in, hidden_ref, sems.at[1]),
        pltpu.make_async_copy(out_w_in, out_w_ref, sems.at[2]),
    ]
    for copy in first + late:
        copy.start()
    for copy in first:
        copy.wait()

    @pl.loop(0, tiles)
    def _(i):
        @pl.when(live_ref[i] > 0)
        def _():
            source = pl.ds(pl.multiple_of(i * TILE, TILE), TILE)
            packed[pl.ds(pl.multiple_of(spot_ref[i] * TILE, TILE), TILE), :] = kv[source, :]

    used = spot_ref[tiles - 1] + live_ref[tiles - 1]
    chunks = (used + per_chunk - 1) // per_chunk

    @pl.loop(used, chunks * per_chunk)
    def _(i):
        packed[pl.ds(pl.multiple_of(i * TILE, TILE), TILE), :] = jnp.zeros((TILE, 2 * KVW), jnp.bfloat16)

    lane_tile = lax.broadcasted_iota(jnp.int32, (128, chunk), 1) // TILE
    widen = (lane_tile == lax.broadcasted_iota(jnp.int32, (128, chunk), 0)).astype(jnp.float32).astype(jnp.bfloat16)
    scale = HEAD ** (-0.5)
    for h in range(KV_HEADS):
        heads = [query_ref[:, (h * GROUPS + g) * HEAD : (h * GROUPS + g + 1) * HEAD] for g in range(GROUPS)]
        query = jnp.concatenate(heads, axis=0)
        top[...] = jnp.full(top.shape, -1e30, jnp.float32)
        total[...] = jnp.zeros(total.shape, jnp.float32)
        acc[...] = jnp.zeros(acc.shape, jnp.float32)

        @pl.loop(0, chunks)
        def _(j):
            keys = packed[pl.ds(pl.multiple_of(j * chunk, 128), chunk), h * HEAD : (h + 1) * HEAD]
            s = lax.dot_general(query, keys, (((1,), (1,)), ((), ())), preferred_element_type=jnp.float32)
            allowed = jnp.dot(allowed_ref[j], widen, preferred_element_type=jnp.float32)
            bias = (allowed - 1.0) * 1e30
            bias = [jnp.broadcast_to(bias[t : t + 1], (TILE, chunk)) for t in range(rows // TILE)]
            bias = jnp.concatenate(bias, axis=0)
            s = s.reshape(GROUPS, rows, chunk) + bias[None]
            s = s.reshape(GROUPS * rows, chunk)
            scores[j] = s
            best = top[...]
            for c in range(0, chunk, 128):
                best = jnp.maximum(best, s[:, c : c + 128])
            top[...] = best

        highest = jnp.max(top[...], axis=1, keepdims=True)
        top[...] = jnp.broadcast_to(highest, top.shape)

        @pl.loop(0, chunks)
        def _(j):
            values = packed[pl.ds(pl.multiple_of(j * chunk, 128), chunk), KVW + h * HEAD : KVW + (h + 1) * HEAD]
            high = top[...]
            s = scores[j]
            parts = []
            running = total[...]
            for c in range(0, chunk, 128):
                w = jnp.exp((s[:, c : c + 128] - high) * scale)
                running = running + w
                parts.append(w.astype(jnp.bfloat16))
            total[...] = running
            weights = jnp.concatenate(parts, axis=1)
            acc[...] += jnp.dot(weights, values, preferred_element_type=jnp.float32)

        denominator = jnp.sum(total[...], axis=1, keepdims=True)
        result = (acc[...] / denominator).astype(jnp.bfloat16)
        for g in range(GROUPS):
            col = (h * GROUPS + g) * HEAD
            attended[:, col : col + HEAD] = result[g * rows : (g + 1) * rows]
    for copy in late:
        copy.wait()
    projected = jnp.dot(attended[...], out_w_ref[...], preferred_element_type=jnp.float32)
    attention_ref[...] = projected.astype(jnp.bfloat16)
    residual = (hidden_ref[...].astype(jnp.float32) + projected).astype(jnp.bfloat16)
    residual_ref[...] = residual
    wide = residual.astype(jnp.float32)
    inverse = lax.rsqrt(jnp.mean(wide * wide, axis=-1, keepdims=True) + 1e-05)
    normed = (wide * inverse * gain_ref[...]).astype(jnp.bfloat16)
    slot = lax.broadcasted_iota(jnp.int32, (SLOTS, rows), 0)
    chosen = (slot == target_ref[0:1, :]) | (slot == target_ref[1:2, :])
    selector = chosen.astype(jnp.float32).astype(jnp.bfloat16)
    outgoing_ref[...] = jnp.dot(selector, normed, preferred_element_type=jnp.float32).astype(jnp.bfloat16)


def attend(live, spot, allowed, query, target, out_w, hidden, gain, blocks):
    rows = query.shape[0]
    chunks = allowed.shape[0]
    n = len(blocks)
    chunk = n * rows // chunks
    return pl.pallas_call(
        functools.partial(attend_kernel, n),
        out_shape=[
            jax.ShapeDtypeStruct((rows, D), jnp.bfloat16),
            jax.ShapeDtypeStruct((rows, D), jnp.bfloat16),
            jax.ShapeDtypeStruct((SLOTS, D), jnp.bfloat16),
        ],
        in_specs=[SMEM, SMEM, VMEM, ANY, VMEM, ANY, ANY, VMEM] + [ANY] * n,
        out_specs=[VMEM] * 3,
        scratch_shapes=[
            pltpu.VMEM((rows, D), jnp.bfloat16),
            pltpu.VMEM((D, D), jnp.bfloat16),
            pltpu.VMEM((rows, D), jnp.bfloat16),
            pltpu.VMEM((n * rows, 2 * KVW), jnp.bfloat16),
            pltpu.VMEM((n * rows, 2 * KVW), jnp.bfloat16),
            pltpu.VMEM((chunks, GROUPS * rows, chunk), jnp.float32),
            pltpu.VMEM((GROUPS * rows, HEAD), jnp.float32),
            pltpu.VMEM((GROUPS * rows, HEAD), jnp.float32),
            pltpu.VMEM((GROUPS * rows, HEAD), jnp.float32),
            pltpu.VMEM((rows, D), jnp.bfloat16),
            pltpu.SemaphoreType.DMA((3 + n,)),
        ],
        compiler_params=pltpu.CompilerParams(vmem_limit_bytes=56 * MB),
        name="attend",
    )(live, spot, allowed, query, target, out_w, hidden, gain, *blocks)


def key_order(tile_mask, me, world):
    tiles, count = tile_mask.shape
    order = me ^ jnp.arange(world)
    mask = jnp.take(tile_mask.reshape(tiles, world, tiles), order, axis=1, mode="clip").reshape(tiles, count)
    mask = (mask > 0).astype(jnp.bfloat16)
    live = jnp.max(mask, axis=0)
    index = jnp.arange(count)
    spot = jnp.dot(live, (index[:, None] < index[None, :]).astype(jnp.bfloat16), preferred_element_type=jnp.float32)
    move = (spot[:, None] == index[None, :].astype(jnp.float32)) & (live[:, None] > 0)
    placed = jnp.dot(mask, move.astype(jnp.bfloat16), preferred_element_type=jnp.float32)
    per_chunk = 2 * tiles
    placed = placed.reshape(tiles, count // per_chunk, per_chunk).transpose(1, 0, 2)
    placed = jnp.pad(placed, ((0, 0), (0, -tiles % 16), (0, 128 - per_chunk))).astype(jnp.bfloat16)
    return live.astype(jnp.int32), spot.astype(jnp.int32), placed


def expert_kernel(planes, shared, cuts, step, group, place_ref, rows_in, *rest):
    count, groups = planes * shared, len(group)
    pieces, out_refs = rest[:count], rest[count : count + groups]
    loaded, rows_ref, full, total, sems = rest[count + groups :]
    depth = pieces[0].shape[1]
    plane, seat = place_ref[0], place_ref[1]
    loads = [
        pltpu.make_async_copy(rows_in.at[place_ref[2] ^ j], loaded.at[g], sems.at[count * len(cuts) + g])
        for g, j in enumerate(group)
    ]
    copies = []
    for c, (low, high) in enumerate(cuts):
        for n in range(count):
            m, k = divmod(n, planes)
            at = ((plane ^ k) * shared + (seat ^ m)) * depth
            target = full.at[:, pl.ds(pl.multiple_of(at, depth), depth), pl.ds(low, high - low)]
            copies.append(pltpu.make_async_copy(pieces[n].at[:, :, pl.ds(low, high - low)], target, sems.at[c * count + n]))
            copies[-1].start()
        if c == 0:
            for load in loads:
                load.start()
    for load in loads:
        load.wait()
    rows_ref[...] = loaded[...].astype(jnp.float32).reshape(rows_ref.shape).astype(jnp.bfloat16)
    for c, (low, high) in enumerate(cuts):
        for copy in copies[c * count : (c + 1) * count]:
            copy.wait()
        for at in range(low, high, step):
            rows = rows_ref[...]
            gated = jnp.dot(rows, full[0, :, at : at + step], preferred_element_type=jnp.float32)
            upper = jnp.dot(rows, full[1, :, at : at + step], preferred_element_type=jnp.float32)
            hidden = (gated / (1.0 + jnp.exp(-gated)) * upper).astype(jnp.bfloat16)
            part = lax.dot_general(
                hidden, full[2, :, at : at + step], (((1,), (1,)), ((), ())), preferred_element_type=jnp.float32
            )
            if at == 0:
                total[...] = part
            else:
                total[...] += part
    for g in range(groups):
        out_refs[g][...] = total[g * CAP : (g + 1) * CAP, :].astype(jnp.bfloat16)


def run_expert(place, rows, group, pieces, planes, shared):
    depth, ff = pieces[0].shape[1:]
    count, groups = planes * shared, len(group)
    step = 256
    edges = [0, step, 3 * step, 5 * step, ff]
    cuts = list(zip(edges[:-1], edges[1:]))
    return pl.pallas_call(
        functools.partial(expert_kernel, planes, shared, cuts, step, group),
        out_shape=[jax.ShapeDtypeStruct((CAP, D), jnp.bfloat16)] * groups,
        in_specs=[SMEM, ANY] + [ANY] * count,
        out_specs=[VMEM] * groups,
        scratch_shapes=[
            pltpu.VMEM((groups, CAP, D), jnp.bfloat16),
            pltpu.VMEM((groups * CAP, D), jnp.bfloat16),
            pltpu.VMEM((3, D, ff), jnp.bfloat16),
            pltpu.VMEM((groups * CAP, D), jnp.float32),
            pltpu.SemaphoreType.DMA((count * len(cuts) + groups,)),
        ],
        compiler_params=pltpu.CompilerParams(vmem_limit_bytes=60 * MB),
        cost_estimate=pl.CostEstimate(
            flops=6 * groups * CAP * D * ff, bytes_accessed=3 * D * ff * 2, transcendentals=groups * CAP * ff
        ),
        name="expert",
    )(place, rows, *pieces)


def combine_kernel(target_ref, probs_ref, residual_ref, *rest):
    returned_refs, out_ref = rest[:-1], rest[-1]
    rows = residual_ref.shape[0]
    slot = lax.broadcasted_iota(jnp.int32, (rows, CAP), 1)
    picked = jnp.zeros((TOP * rows, D), jnp.float32)
    for j, returned_ref in enumerate(returned_refs):
        selector = [(slot + j * CAP == target_ref[:, k : k + 1]).astype(jnp.float32) for k in range(TOP)]
        selector = jnp.concatenate(selector, axis=0).astype(jnp.bfloat16)
        picked = picked + jnp.dot(selector, returned_ref[...], preferred_element_type=jnp.float32)
    total = jnp.zeros((rows, D), jnp.float32)
    for k in range(TOP):
        total = total + picked[k * rows : (k + 1) * rows] * probs_ref[:, k : k + 1]
    out_ref[...] = (residual_ref[...].astype(jnp.float32) + total).astype(jnp.bfloat16)


def combine(returned, target, probs, residual):
    return pl.pallas_call(
        combine_kernel,
        out_shape=jax.ShapeDtypeStruct(residual.shape, jnp.bfloat16),
        in_specs=[VMEM] * (3 + len(returned)),
        out_specs=VMEM,
        compiler_params=pltpu.CompilerParams(vmem_limit_bytes=24 * MB),
        name="combine",
    )(target, probs, residual, *returned)


def places_of(ids):
    rows = ids.shape[0]
    onehot = (ids[:, :, None] == jnp.arange(EXPERTS, dtype=jnp.int32)).astype(jnp.float32)
    named = jnp.sum(onehot, axis=1)
    earlier = (jnp.arange(rows)[:, None] > jnp.arange(rows)[None, :]).astype(jnp.bfloat16)
    before = jnp.dot(earlier, named.astype(jnp.bfloat16), preferred_element_type=jnp.float32)
    slot = jnp.sum(onehot * before[:, None, :], axis=2).astype(jnp.int32)
    return slot


def shards(
    planes,
    shared,
    hidden_in,
    queries,
    key_proj,
    value_proj,
    tile_mask,
    out_weight,
    moe_gain,
    gate_weight,
    up_weight,
    down_weight,
    expert_ids,
    gate_probs,
):
    ctx = ("plane", "seat")
    world = planes * shared
    plane = lax.axis_index("plane")
    seat = lax.axis_index("seat")
    me = plane * shared + seat
    mine = lax.axis_index("exp") * planes + plane
    place = jnp.stack([plane, seat, mine]).astype(jnp.int32)

    def swap(x, bit):
        return lax.ppermute(x, ctx, [(i, i ^ bit) for i in range(world)])

    def tie(value, places):
        places = [at for at in places if at in pieces]
        value, found = lax.optimization_barrier((value, [pieces[at] for at in places]))
        pieces.update(zip(places, found))
        return value

    ids = expert_ids[0]
    spot = places_of(ids)
    target = ids * CAP + spot
    back = (ids ^ mine) * CAP + spot
    order = key_order(tile_mask[0], me, world)
    own = jnp.concatenate([key_proj[0], value_proj[0]], axis=1)
    bit = world // 2
    half = shared // 2
    blocks = {0: own, bit: swap(own, bit)}
    packed = pack(place, gate_weight, up_weight, down_weight)
    far = [k for k in range(planes) if k >= planes // 2 and k]
    near = [k for k in range(planes) if k < planes // 2 and k]
    pieces = {(0, 0): packed[0]}
    for k in far[:1] + near:
        pieces[0, k] = swap(packed[k], k * shared)
    pieces[half, 0] = swap(packed[0], half)
    bit //= 2
    while bit:
        if bit == 1:
            last = world - 2
            blocks[last] = tie(blocks[last], [(2, 0)])
            blocks[last], order, target, back = lax.optimization_barrier((blocks[last], order, target, back))
            if far:
                early = half + shared
                blocks[early], second = lax.optimization_barrier((blocks[early], packed[far[1]]))
                pieces[0, far[1]] = swap(second, far[1] * shared)
        blocks.update({m | bit: swap(x, bit) for m, x in list(blocks.items())})
        bit //= 2
    blocks = tie(blocks, [(0, 2)])
    bit = half
    while bit:
        for (m, k), x in list(pieces.items()):
            if (m | bit, k) not in pieces:
                pieces[m | bit, k] = swap(x, bit)
        bit //= 2

    live, where, allowed = order
    attention_out, residual, outgoing = attend(
        live,
        where,
        allowed,
        queries[0],
        target.T,
        out_weight,
        hidden_in[0],
        moe_gain[None],
        [blocks[m] for m in range(world)],
    )
    outgoing = tie(outgoing, [(2, 2)])
    arrived = lax.all_to_all(
        outgoing.reshape(EXPERTS, CAP, D), ("exp", "plane"), split_axis=0, concat_axis=0, tiled=True
    )
    weights = [pieces[m, k] for m in range(shared) for k in range(planes)]
    first = [j for j in range(EXPERTS) if planes > 1 and j % planes >= planes // 2]
    first += [j for j in range(planes, EXPERTS) if j not in first]
    second = [j for j in range(EXPERTS) if j not in first]
    returned = {}
    for group in (first, second):
        for j, x in zip(group, run_expert(place, arrived, group, weights, planes, shared)):
            step = j % planes * (EXPERTS // planes) + j // planes
            pairs = [(i, i ^ step) for i in range(EXPERTS)]
            returned[j] = lax.ppermute(x, ("plane", "exp"), pairs) if j else x
    layer_out = combine([returned[j] for j in range(EXPERTS)], back, gate_probs[0], residual)
    return attention_out[None], layer_out[None]


def solution(mesh):
    n_ctx, n_exp = mesh.shape["ctx"], mesh.shape["exp"]
    planes = EXPERTS // n_exp
    shared = n_ctx // planes
    fine = Mesh(mesh.devices.reshape(planes, shared, n_exp), ("plane", "seat", "exp"))
    split = P("exp", ("plane", "seat"), None)
    return jax.shard_map(
        functools.partial(shards, planes, shared),
        mesh=fine,
        in_specs=(split, split, split, split, split, P(), P(), split, split, split, split, split),
        out_specs=(split, split),
        check_vma=False,
    )
```

```python
import functools

import jax
import jax.numpy as jnp
from jax import lax
from jax.experimental import pallas as pl
from jax.experimental.pallas import tpu as pltpu
from jax.sharding import Mesh, PartitionSpec as P

D = 1024
HEADS = 8
KV_HEADS = 2
EXPERTS = 8
TOP = 2
TILE = 32
CAP = 72
HEAD = D // HEADS
GROUPS = HEADS // KV_HEADS
KVW = KV_HEADS * HEAD
SLOTS = EXPERTS * CAP
MB = 1 << 20

VMEM = pl.BlockSpec(memory_space=pltpu.VMEM)
SMEM = pl.BlockSpec(memory_space=pltpu.SMEM)
ANY = pl.BlockSpec(memory_space=pl.ANY)


def pack_kernel(planes, place_ref, gate_ref, up_ref, down_ref, *rest):
    outs, sems = rest[:planes], rest[planes]
    plane = place_ref[0]
    copies = []
    for k in range(planes):
        owner = plane ^ k
        for w, ref in enumerate((gate_ref, up_ref, down_ref)):
            copies.append(pltpu.make_async_copy(ref.at[owner], outs[k].at[w], sems.at[3 * k + w]))
    for copy in copies:
        copy.start()
    for copy in copies:
        copy.wait()


def pack(place, gate, up, down):
    planes, rows, ff = gate.shape
    return pl.pallas_call(
        functools.partial(pack_kernel, planes),
        out_shape=[jax.ShapeDtypeStruct((3, rows, ff), gate.dtype)] * planes,
        in_specs=[SMEM, ANY, ANY, ANY],
        out_specs=[VMEM] * planes,
        scratch_shapes=[pltpu.SemaphoreType.DMA((3 * planes,))],
        name="pack_weights",
    )(place, gate, up, down)


def attend_kernel(blocks, live_ref, spot_ref, allowed_ref, query_in, target_ref, out_w_in, hidden_in, gain_ref, *rest):
    kv_in = rest[:blocks]
    attention_ref, residual_ref, outgoing_ref = rest[blocks : blocks + 3]
    query_ref, out_w_ref, hidden_ref, kv, packed, scores, top, total, acc, attended, sems = rest[blocks + 3 :]
    rows = query_ref.shape[0]
    chunk = scores.shape[2]
    tiles = live_ref.shape[0]
    per_chunk = chunk // TILE
    first = [pltpu.make_async_copy(query_in, query_ref, sems.at[0])]
    for i in range(blocks):
        first.append(pltpu.make_async_copy(kv_in[i], kv.at[pl.ds(i * rows, rows)], sems.at[3 + i]))
    late = [
        pltpu.make_async_copy(hidden_in, hidden_ref, sems.at[1]),
        pltpu.make_async_copy(out_w_in, out_w_ref, sems.at[2]),
    ]
    for copy in first + late:
        copy.start()
    for copy in first:
        copy.wait()

    @pl.loop(0, tiles)
    def _(i):
        @pl.when(live_ref[i] > 0)
        def _():
            source = pl.ds(pl.multiple_of(i * TILE, TILE), TILE)
            packed[pl.ds(pl.multiple_of(spot_ref[i] * TILE, TILE), TILE), :] = kv[source, :]

    used = spot_ref[tiles - 1] + live_ref[tiles - 1]
    chunks = (used + per_chunk - 1) // per_chunk

    @pl.loop(used, chunks * per_chunk)
    def _(i):
        packed[pl.ds(pl.multiple_of(i * TILE, TILE), TILE), :] = jnp.zeros((TILE, 2 * KVW), jnp.bfloat16)

    lane_tile = lax.broadcasted_iota(jnp.int32, (128, chunk), 1) // TILE
    widen = (lane_tile == lax.broadcasted_iota(jnp.int32, (128, chunk), 0)).astype(jnp.float32).astype(jnp.bfloat16)
    scale = HEAD ** (-0.5)
    for h in range(KV_HEADS):
        heads = [query_ref[:, (h * GROUPS + g) * HEAD : (h * GROUPS + g + 1) * HEAD] for g in range(GROUPS)]
        query = jnp.concatenate(heads, axis=0)
        top[...] = jnp.full(top.shape, -1e30, jnp.float32)
        total[...] = jnp.zeros(total.shape, jnp.float32)
        acc[...] = jnp.zeros(acc.shape, jnp.float32)

        @pl.loop(0, chunks)
        def _(j):
            keys = packed[pl.ds(pl.multiple_of(j * chunk, 128), chunk), h * HEAD : (h + 1) * HEAD]
            s = lax.dot_general(query, keys, (((1,), (1,)), ((), ())), preferred_element_type=jnp.float32)
            allowed = jnp.dot(allowed_ref[j], widen, preferred_element_type=jnp.float32)
            bias = (allowed - 1.0) * 1e30
            bias = [jnp.broadcast_to(bias[t : t + 1], (TILE, chunk)) for t in range(rows // TILE)]
            bias = jnp.concatenate(bias, axis=0)
            s = s.reshape(GROUPS, rows, chunk) + bias[None]
            s = s.reshape(GROUPS * rows, chunk)
            scores[j] = s
            best = top[...]
            for c in range(0, chunk, 128):
                best = jnp.maximum(best, s[:, c : c + 128])
            top[...] = best

        highest = jnp.max(top[...], axis=1, keepdims=True)
        top[...] = jnp.broadcast_to(highest, top.shape)

        @pl.loop(0, chunks)
        def _(j):
            values = packed[pl.ds(pl.multiple_of(j * chunk, 128), chunk), KVW + h * HEAD : KVW + (h + 1) * HEAD]
            high = top[...]
            s = scores[j]
            parts = []
            running = total[...]
            for c in range(0, chunk, 128):
                w = jnp.exp((s[:, c : c + 128] - high) * scale)
                running = running + w
                parts.append(w.astype(jnp.bfloat16))
            total[...] = running
            weights = jnp.concatenate(parts, axis=1)
            acc[...] += jnp.dot(weights, values, preferred_element_type=jnp.float32)

        denominator = jnp.sum(total[...], axis=1, keepdims=True)
        result = (acc[...] / denominator).astype(jnp.bfloat16)
        for g in range(GROUPS):
            col = (h * GROUPS + g) * HEAD
            attended[:, col : col + HEAD] = result[g * rows : (g + 1) * rows]
    for copy in late:
        copy.wait()
    projected = jnp.dot(attended[...], out_w_ref[...], preferred_element_type=jnp.float32)
    attention_ref[...] = projected.astype(jnp.bfloat16)
    residual = (hidden_ref[...].astype(jnp.float32) + projected).astype(jnp.bfloat16)
    residual_ref[...] = residual
    wide = residual.astype(jnp.float32)
    inverse = lax.rsqrt(jnp.mean(wide * wide, axis=-1, keepdims=True) + 1e-05)
    normed = (wide * inverse * gain_ref[...]).astype(jnp.bfloat16)
    slot = lax.broadcasted_iota(jnp.int32, (SLOTS, rows), 0)
    chosen = (slot == target_ref[0:1, :]) | (slot == target_ref[1:2, :])
    selector = chosen.astype(jnp.float32).astype(jnp.bfloat16)
    outgoing_ref[...] = jnp.dot(selector, normed, preferred_element_type=jnp.float32).astype(jnp.bfloat16)


def attend(live, spot, allowed, query, target, out_w, hidden, gain, blocks):
    rows = query.shape[0]
    chunks = allowed.shape[0]
    n = len(blocks)
    chunk = n * rows // chunks
    return pl.pallas_call(
        functools.partial(attend_kernel, n),
        out_shape=[
            jax.ShapeDtypeStruct((rows, D), jnp.bfloat16),
            jax.ShapeDtypeStruct((rows, D), jnp.bfloat16),
            jax.ShapeDtypeStruct((SLOTS, D), jnp.bfloat16),
        ],
        in_specs=[SMEM, SMEM, VMEM, ANY, VMEM, ANY, ANY, VMEM] + [ANY] * n,
        out_specs=[VMEM] * 3,
        scratch_shapes=[
            pltpu.VMEM((rows, D), jnp.bfloat16),
            pltpu.VMEM((D, D), jnp.bfloat16),
            pltpu.VMEM((rows, D), jnp.bfloat16),
            pltpu.VMEM((n * rows, 2 * KVW), jnp.bfloat16),
            pltpu.VMEM((n * rows, 2 * KVW), jnp.bfloat16),
            pltpu.VMEM((chunks, GROUPS * rows, chunk), jnp.float32),
            pltpu.VMEM((GROUPS * rows, HEAD), jnp.float32),
            pltpu.VMEM((GROUPS * rows, HEAD), jnp.float32),
            pltpu.VMEM((GROUPS * rows, HEAD), jnp.float32),
            pltpu.VMEM((rows, D), jnp.bfloat16),
            pltpu.SemaphoreType.DMA((3 + n,)),
        ],
        compiler_params=pltpu.CompilerParams(vmem_limit_bytes=56 * MB),
        name="attend",
    )(live, spot, allowed, query, target, out_w, hidden, gain, *blocks)


def key_order(tile_mask, me, world):
    tiles, count = tile_mask.shape
    order = me ^ jnp.arange(world)
    mask = jnp.take(tile_mask.reshape(tiles, world, tiles), order, axis=1, mode="clip").reshape(tiles, count)
    mask = (mask > 0).astype(jnp.bfloat16)
    live = jnp.max(mask, axis=0)
    index = jnp.arange(count)
    spot = jnp.dot(live, (index[:, None] < index[None, :]).astype(jnp.bfloat16), preferred_element_type=jnp.float32)
    move = (spot[:, None] == index[None, :].astype(jnp.float32)) & (live[:, None] > 0)
    placed = jnp.dot(mask, move.astype(jnp.bfloat16), preferred_element_type=jnp.float32)
    per_chunk = 2 * tiles
    placed = placed.reshape(tiles, count // per_chunk, per_chunk).transpose(1, 0, 2)
    placed = jnp.pad(placed, ((0, 0), (0, -tiles % 16), (0, 128 - per_chunk))).astype(jnp.bfloat16)
    return live.astype(jnp.int32), spot.astype(jnp.int32), placed


def expert_kernel(planes, shared, cuts, step, group, place_ref, rows_in, *rest):
    count, groups = planes * shared, len(group)
    pieces, out_refs = rest[:count], rest[count : count + groups]
    loaded, rows_ref, full, total, sems = rest[count + groups :]
    depth = pieces[0].shape[1]
    plane, seat = place_ref[0], place_ref[1]
    loads = [
        pltpu.make_async_copy(rows_in.at[place_ref[2] ^ j], loaded.at[g], sems.at[count * len(cuts) + g])
        for g, j in enumerate(group)
    ]
    copies = []
    for c, (low, high) in enumerate(cuts):
        for n in range(count):
            m, k = divmod(n, planes)
            at = ((plane ^ k) * shared + (seat ^ m)) * depth
            target = full.at[:, pl.ds(pl.multiple_of(at, depth), depth), pl.ds(low, high - low)]
            copies.append(pltpu.make_async_copy(pieces[n].at[:, :, pl.ds(low, high - low)], target, sems.at[c * count + n]))
            copies[-1].start()
        if c == 0:
            for load in loads:
                load.start()
    for load in loads:
        load.wait()
    rows_ref[...] = loaded[...].astype(jnp.float32).reshape(rows_ref.shape).astype(jnp.bfloat16)
    for c, (low, high) in enumerate(cuts):
        for copy in copies[c * count : (c + 1) * count]:
            copy.wait()
        for at in range(low, high, step):
            rows = rows_ref[...]
            gated = jnp.dot(rows, full[0, :, at : at + step], preferred_element_type=jnp.float32)
            upper = jnp.dot(rows, full[1, :, at : at + step], preferred_element_type=jnp.float32)
            hidden = (gated / (1.0 + jnp.exp(-gated)) * upper).astype(jnp.bfloat16)
            part = lax.dot_general(
                hidden, full[2, :, at : at + step], (((1,), (1,)), ((), ())), preferred_element_type=jnp.float32
            )
            if at == 0:
                total[...] = part
            else:
                total[...] += part
    for g in range(groups):
        out_refs[g][...] = total[g * CAP : (g + 1) * CAP, :].astype(jnp.bfloat16)


def run_expert(place, rows, group, pieces, planes, shared):
    depth, ff = pieces[0].shape[1:]
    count, groups = planes * shared, len(group)
    step = 256
    edges = [0, step, 3 * step, 5 * step, ff]
    cuts = list(zip(edges[:-1], edges[1:]))
    return pl.pallas_call(
        functools.partial(expert_kernel, planes, shared, cuts, step, group),
        out_shape=[jax.ShapeDtypeStruct((CAP, D), jnp.bfloat16)] * groups,
        in_specs=[SMEM, ANY] + [ANY] * count,
        out_specs=[VMEM] * groups,
        scratch_shapes=[
            pltpu.VMEM((groups, CAP, D), jnp.bfloat16),
            pltpu.VMEM((groups * CAP, D), jnp.bfloat16),
            pltpu.VMEM((3, D, ff), jnp.bfloat16),
            pltpu.VMEM((groups * CAP, D), jnp.float32),
            pltpu.SemaphoreType.DMA((count * len(cuts) + groups,)),
        ],
        compiler_params=pltpu.CompilerParams(vmem_limit_bytes=60 * MB),
        cost_estimate=pl.CostEstimate(
            flops=6 * groups * CAP * D * ff, bytes_accessed=3 * D * ff * 2, transcendentals=groups * CAP * ff
        ),
        name="expert",
    )(place, rows, *pieces)


def combine_kernel(target_ref, probs_ref, residual_ref, own_in, *rest):
    returned_refs, out_ref, own_ref, sem = rest[:-3], rest[-3], rest[-2], rest[-1]
    load = pltpu.make_async_copy(own_in, own_ref, sem.at[0])
    load.start()
    rows = residual_ref.shape[0]
    load.wait()
    slot = lax.broadcasted_iota(jnp.int32, (rows, EXPERTS * CAP), 1)
    parts = [own_ref[...], *[ref[...] for ref in returned_refs]]
    parts = jnp.concatenate([part.astype(jnp.float32) for part in parts], axis=0).astype(jnp.bfloat16)
    selector = [(slot == target_ref[:, k : k + 1]).astype(jnp.float32) for k in range(TOP)]
    selector = jnp.concatenate(selector, axis=0).astype(jnp.bfloat16)
    picked = jnp.dot(selector, parts, preferred_element_type=jnp.float32)
    total = jnp.zeros((rows, D), jnp.float32)
    for k in range(TOP):
        total = total + picked[k * rows : (k + 1) * rows] * probs_ref[:, k : k + 1]
    out_ref[...] = (residual_ref[...].astype(jnp.float32) + total).astype(jnp.bfloat16)


def combine(returned, target, probs, residual):
    return pl.pallas_call(
        combine_kernel,
        out_shape=jax.ShapeDtypeStruct(residual.shape, jnp.bfloat16),
        in_specs=[VMEM] * 3 + [ANY] + [VMEM] * (len(returned) - 1),
        out_specs=VMEM,
        scratch_shapes=[pltpu.VMEM((CAP, D), jnp.bfloat16), pltpu.SemaphoreType.DMA((1,))],
        compiler_params=pltpu.CompilerParams(vmem_limit_bytes=24 * MB),
        name="combine",
    )(target, probs, residual, *returned)


def places_of(ids):
    rows = ids.shape[0]
    onehot = (ids[:, :, None] == jnp.arange(EXPERTS, dtype=jnp.int32)).astype(jnp.float32)
    named = jnp.sum(onehot, axis=1)
    earlier = (jnp.arange(rows)[:, None] > jnp.arange(rows)[None, :]).astype(jnp.bfloat16)
    before = jnp.dot(earlier, named.astype(jnp.bfloat16), preferred_element_type=jnp.float32)
    slot = jnp.sum(onehot * before[:, None, :], axis=2).astype(jnp.int32)
    return slot


def shards(
    planes,
    shared,
    hidden_in,
    queries,
    key_proj,
    value_proj,
    tile_mask,
    out_weight,
    moe_gain,
    gate_weight,
    up_weight,
    down_weight,
    expert_ids,
    gate_probs,
):
    ctx = ("plane", "seat")
    world = planes * shared
    plane = lax.axis_index("plane")
    seat = lax.axis_index("seat")
    me = plane * shared + seat
    mine = lax.axis_index("exp") * planes + plane
    place = jnp.stack([plane, seat, mine]).astype(jnp.int32)

    def swap(x, bit):
        return lax.ppermute(x, ctx, [(i, i ^ bit) for i in range(world)])

    def tie(value, places):
        places = [at for at in places if at in pieces]
        value, found = lax.optimization_barrier((value, [pieces[at] for at in places]))
        pieces.update(zip(places, found))
        return value

    ids = expert_ids[0]
    spot = places_of(ids)
    target = ids * CAP + spot
    back = (ids ^ mine) * CAP + spot
    order = key_order(tile_mask[0], me, world)
    own = jnp.concatenate([key_proj[0], value_proj[0]], axis=1)
    bit = world // 2
    half = shared // 2
    blocks = {0: own, bit: swap(own, bit)}
    packed = pack(place, gate_weight, up_weight, down_weight)
    far = [k for k in range(planes) if k >= planes // 2 and k]
    near = [k for k in range(planes) if k < planes // 2 and k]
    pieces = {(0, 0): packed[0]}
    for k in far[:1] + near:
        pieces[0, k] = swap(packed[k], k * shared)
    pieces[half, 0] = swap(packed[0], half)
    bit //= 2
    while bit:
        if bit == 1:
            last = world - 2
            blocks[last] = tie(blocks[last], [(2, 0)])
            blocks[last], order, target, back = lax.optimization_barrier((blocks[last], order, target, back))
            if far:
                early = half + shared
                blocks[early], second = lax.optimization_barrier((blocks[early], packed[far[1]]))
                pieces[0, far[1]] = swap(second, far[1] * shared)
        blocks.update({m | bit: swap(x, bit) for m, x in list(blocks.items())})
        bit //= 2
    blocks = tie(blocks, [(0, 2)])
    bit = half
    while bit:
        for (m, k), x in list(pieces.items()):
            if (m | bit, k) not in pieces:
                pieces[m | bit, k] = swap(x, bit)
        bit //= 2

    live, where, allowed = order
    attention_out, residual, outgoing = attend(
        live,
        where,
        allowed,
        queries[0],
        target.T,
        out_weight,
        hidden_in[0],
        moe_gain[None],
        [blocks[m] for m in range(world)],
    )
    outgoing = tie(outgoing, [(2, 2)])
    arrived = lax.all_to_all(
        outgoing.reshape(EXPERTS, CAP, D), ("exp", "plane"), split_axis=0, concat_axis=0, tiled=True
    )
    weights = [pieces[m, k] for m in range(shared) for k in range(planes)]
    first = [j for j in range(EXPERTS) if planes > 1 and j % planes >= planes // 2]
    first += [j for j in range(planes, EXPERTS) if j not in first]
    second = [j for j in range(EXPERTS) if j not in first]
    returned = {}
    for group in (first, second):
        for j, x in zip(group, run_expert(place, arrived, group, weights, planes, shared)):
            step = j % planes * (EXPERTS // planes) + j // planes
            pairs = [(i, i ^ step) for i in range(EXPERTS)]
            returned[j] = lax.ppermute(x, ("plane", "exp"), pairs) if j else x
    layer_out = combine([returned[j] for j in range(EXPERTS)], back, gate_probs[0], residual)
    return attention_out[None], layer_out[None]


def solution(mesh):
    n_ctx, n_exp = mesh.shape["ctx"], mesh.shape["exp"]
    planes = EXPERTS // n_exp
    shared = n_ctx // planes
    fine = Mesh(mesh.devices.reshape(planes, shared, n_exp), ("plane", "seat", "exp"))
    split = P("exp", ("plane", "seat"), None)
    return jax.shard_map(
        functools.partial(shards, planes, shared),
        mesh=fine,
        in_specs=(split, split, split, split, split, P(), P(), split, split, split, split, split),
        out_specs=(split, split),
        check_vma=False,
    )
```

```python
import functools

import jax
import jax.numpy as jnp
from jax import lax
from jax.experimental import pallas as pl
from jax.experimental.pallas import tpu as pltpu
from jax.sharding import Mesh, PartitionSpec as P

D = 1024
HEADS = 8
KV_HEADS = 2
EXPERTS = 8
TOP = 2
TILE = 32
CAP = 72
HEAD = D // HEADS
GROUPS = HEADS // KV_HEADS
KVW = KV_HEADS * HEAD
SLOTS = EXPERTS * CAP
MB = 1 << 20

VMEM = pl.BlockSpec(memory_space=pltpu.VMEM)
SMEM = pl.BlockSpec(memory_space=pltpu.SMEM)
ANY = pl.BlockSpec(memory_space=pl.ANY)


def pack_kernel(planes, place_ref, gate_ref, up_ref, down_ref, *rest):
    outs, sems = rest[:planes], rest[planes]
    plane = place_ref[0]
    copies = []
    for k in range(planes):
        owner = plane ^ k
        for w, ref in enumerate((gate_ref, up_ref, down_ref)):
            copies.append(pltpu.make_async_copy(ref.at[owner], outs[k].at[w], sems.at[3 * k + w]))
    for copy in copies:
        copy.start()
    for copy in copies:
        copy.wait()


def pack(place, gate, up, down):
    planes, rows, ff = gate.shape
    return pl.pallas_call(
        functools.partial(pack_kernel, planes),
        out_shape=[jax.ShapeDtypeStruct((3, rows, ff), gate.dtype)] * planes,
        in_specs=[SMEM, ANY, ANY, ANY],
        out_specs=[VMEM] * planes,
        scratch_shapes=[pltpu.SemaphoreType.DMA((3 * planes,))],
        name="pack_weights",
    )(place, gate, up, down)


def attend_kernel(blocks, live_ref, spot_ref, allowed_ref, query_in, target_ref, out_w_in, hidden_in, gain_ref, *rest):
    kv_in = rest[:blocks]
    attention_ref, residual_ref, outgoing_ref = rest[blocks : blocks + 3]
    query_ref, out_w_ref, hidden_ref, kv, packed, scores, top, total, acc, attended, sems = rest[blocks + 3 :]
    rows = query_ref.shape[0]
    chunk = scores.shape[2]
    tiles = live_ref.shape[0]
    per_chunk = chunk // TILE
    first = [pltpu.make_async_copy(query_in, query_ref, sems.at[0])]
    for i in range(blocks):
        first.append(pltpu.make_async_copy(kv_in[i], kv.at[pl.ds(i * rows, rows)], sems.at[3 + i]))
    late = [
        pltpu.make_async_copy(hidden_in, hidden_ref, sems.at[1]),
        pltpu.make_async_copy(out_w_in, out_w_ref, sems.at[2]),
    ]
    for copy in first + late:
        copy.start()
    for copy in first:
        copy.wait()

    @pl.loop(0, tiles)
    def _(i):
        @pl.when(live_ref[i] > 0)
        def _():
            source = pl.ds(pl.multiple_of(i * TILE, TILE), TILE)
            packed[pl.ds(pl.multiple_of(spot_ref[i] * TILE, TILE), TILE), :] = kv[source, :]

    used = spot_ref[tiles - 1] + live_ref[tiles - 1]
    chunks = (used + per_chunk - 1) // per_chunk

    @pl.loop(used, chunks * per_chunk)
    def _(i):
        packed[pl.ds(pl.multiple_of(i * TILE, TILE), TILE), :] = jnp.zeros((TILE, 2 * KVW), jnp.bfloat16)

    lane_tile = lax.broadcasted_iota(jnp.int32, (128, chunk), 1) // TILE
    widen = (lane_tile == lax.broadcasted_iota(jnp.int32, (128, chunk), 0)).astype(jnp.float32).astype(jnp.bfloat16)
    scale = HEAD ** (-0.5)
    for h in range(KV_HEADS):
        heads = [query_ref[:, (h * GROUPS + g) * HEAD : (h * GROUPS + g + 1) * HEAD] for g in range(GROUPS)]
        query = jnp.concatenate(heads, axis=0)
        top[...] = jnp.full(top.shape, -1e30, jnp.float32)
        total[...] = jnp.zeros(total.shape, jnp.float32)
        acc[...] = jnp.zeros(acc.shape, jnp.float32)

        @pl.loop(0, chunks)
        def _(j):
            keys = packed[pl.ds(pl.multiple_of(j * chunk, 128), chunk), h * HEAD : (h + 1) * HEAD]
            s = lax.dot_general(query, keys, (((1,), (1,)), ((), ())), preferred_element_type=jnp.float32)
            allowed = jnp.dot(allowed_ref[j], widen, preferred_element_type=jnp.float32)
            bias = (allowed - 1.0) * 1e30
            bias = [jnp.broadcast_to(bias[t : t + 1], (TILE, chunk)) for t in range(rows // TILE)]
            bias = jnp.concatenate(bias, axis=0)
            s = s.reshape(GROUPS, rows, chunk) + bias[None]
            s = s.reshape(GROUPS * rows, chunk)
            scores[j] = s
            best = top[...]
            for c in range(0, chunk, 128):
                best = jnp.maximum(best, s[:, c : c + 128])
            top[...] = best

        highest = jnp.max(top[...], axis=1, keepdims=True)
        top[...] = jnp.broadcast_to(highest, top.shape)

        @pl.loop(0, chunks)
        def _(j):
            values = packed[pl.ds(pl.multiple_of(j * chunk, 128), chunk), KVW + h * HEAD : KVW + (h + 1) * HEAD]
            high = top[...]
            s = scores[j]
            parts = []
            running = total[...]
            for c in range(0, chunk, 128):
                w = jnp.exp((s[:, c : c + 128] - high) * scale)
                running = running + w
                parts.append(w.astype(jnp.bfloat16))
            total[...] = running
            weights = jnp.concatenate(parts, axis=1)
            acc[...] += jnp.dot(weights, values, preferred_element_type=jnp.float32)

        denominator = jnp.sum(total[...], axis=1, keepdims=True)
        result = (acc[...] / denominator).astype(jnp.bfloat16)
        for g in range(GROUPS):
            col = (h * GROUPS + g) * HEAD
            attended[:, col : col + HEAD] = result[g * rows : (g + 1) * rows]
    for copy in late:
        copy.wait()
    projected = jnp.dot(attended[...], out_w_ref[...], preferred_element_type=jnp.float32)
    attention_ref[...] = projected.astype(jnp.bfloat16)
    residual = (hidden_ref[...].astype(jnp.float32) + projected).astype(jnp.bfloat16)
    residual_ref[...] = residual
    wide = residual.astype(jnp.float32)
    inverse = lax.rsqrt(jnp.mean(wide * wide, axis=-1, keepdims=True) + 1e-05)
    normed = (wide * inverse * gain_ref[...]).astype(jnp.bfloat16)
    slot = lax.broadcasted_iota(jnp.int32, (SLOTS, rows), 0)
    chosen = (slot == target_ref[0:1, :]) | (slot == target_ref[1:2, :])
    selector = chosen.astype(jnp.float32).astype(jnp.bfloat16)
    outgoing_ref[...] = jnp.dot(selector, normed, preferred_element_type=jnp.float32).astype(jnp.bfloat16)


def attend(live, spot, allowed, query, target, out_w, hidden, gain, blocks):
    rows = query.shape[0]
    chunks = allowed.shape[0]
    n = len(blocks)
    chunk = n * rows // chunks
    return pl.pallas_call(
        functools.partial(attend_kernel, n),
        out_shape=[
            jax.ShapeDtypeStruct((rows, D), jnp.bfloat16),
            jax.ShapeDtypeStruct((rows, D), jnp.bfloat16),
            jax.ShapeDtypeStruct((SLOTS, D), jnp.bfloat16),
        ],
        in_specs=[SMEM, SMEM, VMEM, ANY, VMEM, ANY, ANY, VMEM] + [ANY] * n,
        out_specs=[VMEM] * 3,
        scratch_shapes=[
            pltpu.VMEM((rows, D), jnp.bfloat16),
            pltpu.VMEM((D, D), jnp.bfloat16),
            pltpu.VMEM((rows, D), jnp.bfloat16),
            pltpu.VMEM((n * rows, 2 * KVW), jnp.bfloat16),
            pltpu.VMEM((n * rows, 2 * KVW), jnp.bfloat16),
            pltpu.VMEM((chunks, GROUPS * rows, chunk), jnp.float32),
            pltpu.VMEM((GROUPS * rows, HEAD), jnp.float32),
            pltpu.VMEM((GROUPS * rows, HEAD), jnp.float32),
            pltpu.VMEM((GROUPS * rows, HEAD), jnp.float32),
            pltpu.VMEM((rows, D), jnp.bfloat16),
            pltpu.SemaphoreType.DMA((3 + n,)),
        ],
        compiler_params=pltpu.CompilerParams(vmem_limit_bytes=56 * MB),
        name="attend",
    )(live, spot, allowed, query, target, out_w, hidden, gain, *blocks)


def key_order(tile_mask, me, world):
    tiles, count = tile_mask.shape
    order = me ^ jnp.arange(world)
    mask = jnp.take(tile_mask.reshape(tiles, world, tiles), order, axis=1, mode="clip").reshape(tiles, count)
    mask = (mask > 0).astype(jnp.bfloat16)
    live = jnp.max(mask, axis=0)
    index = jnp.arange(count)
    spot = jnp.dot(live, (index[:, None] < index[None, :]).astype(jnp.bfloat16), preferred_element_type=jnp.float32)
    move = (spot[:, None] == index[None, :].astype(jnp.float32)) & (live[:, None] > 0)
    placed = jnp.dot(mask, move.astype(jnp.bfloat16), preferred_element_type=jnp.float32)
    per_chunk = 2 * tiles
    placed = placed.reshape(tiles, count // per_chunk, per_chunk).transpose(1, 0, 2)
    placed = jnp.pad(placed, ((0, 0), (0, -tiles % 16), (0, 128 - per_chunk))).astype(jnp.bfloat16)
    return live.astype(jnp.int32), spot.astype(jnp.int32), placed


def expert_kernel(planes, shared, cuts, step, group, place_ref, rows_in, *rest):
    count, groups = planes * shared, len(group)
    pieces, out_refs = rest[:count], rest[count : count + groups]
    rows_ref, full, total, sems = rest[count + groups :]
    depth = pieces[0].shape[1]
    plane, seat = place_ref[0], place_ref[1]
    copies = []
    for c, (low, high) in enumerate(cuts):
        for n in range(count):
            m, k = divmod(n, planes)
            at = ((plane ^ k) * shared + (seat ^ m)) * depth
            target = full.at[:, pl.ds(pl.multiple_of(at, depth), depth), pl.ds(low, high - low)]
            copies.append(pltpu.make_async_copy(pieces[n].at[:, :, pl.ds(low, high - low)], target, sems.at[c * count + n]))
            copies[-1].start()
    loaded = [rows_in[place_ref[2] ^ j].astype(jnp.float32) for j in group]
    rows_ref[...] = jnp.concatenate(loaded, axis=0).astype(jnp.bfloat16)
    for c, (low, high) in enumerate(cuts):
        for copy in copies[c * count : (c + 1) * count]:
            copy.wait()
        for at in range(low, high, step):
            rows = rows_ref[...]
            gated = jnp.dot(rows, full[0, :, at : at + step], preferred_element_type=jnp.float32)
            upper = jnp.dot(rows, full[1, :, at : at + step], preferred_element_type=jnp.float32)
            hidden = (gated / (1.0 + jnp.exp(-gated)) * upper).astype(jnp.bfloat16)
            part = lax.dot_general(
                hidden, full[2, :, at : at + step], (((1,), (1,)), ((), ())), preferred_element_type=jnp.float32
            )
            if at == 0:
                total[...] = part
            else:
                total[...] += part
    for g in range(groups):
        out_refs[g][...] = total[g * CAP : (g + 1) * CAP, :].astype(jnp.bfloat16)


def run_expert(place, rows, group, pieces, planes, shared):
    depth, ff = pieces[0].shape[1:]
    count, groups = planes * shared, len(group)
    step = 256
    edges = [0, step, 3 * step, 5 * step, ff]
    cuts = list(zip(edges[:-1], edges[1:]))
    return pl.pallas_call(
        functools.partial(expert_kernel, planes, shared, cuts, step, group),
        out_shape=[jax.ShapeDtypeStruct((CAP, D), jnp.bfloat16)] * groups,
        in_specs=[SMEM, VMEM] + [ANY] * count,
        out_specs=[VMEM] * groups,
        scratch_shapes=[
            pltpu.VMEM((groups * CAP, D), jnp.bfloat16),
            pltpu.VMEM((3, D, ff), jnp.bfloat16),
            pltpu.VMEM((groups * CAP, D), jnp.float32),
            pltpu.SemaphoreType.DMA((count * len(cuts),)),
        ],
        compiler_params=pltpu.CompilerParams(vmem_limit_bytes=56 * MB),
        cost_estimate=pl.CostEstimate(
            flops=6 * groups * CAP * D * ff, bytes_accessed=3 * D * ff * 2, transcendentals=groups * CAP * ff
        ),
        name="expert",
    )(place, rows, *pieces)


def combine_kernel(target_ref, probs_ref, residual_ref, *rest):
    returned_refs, out_ref = rest[:-1], rest[-1]
    rows = residual_ref.shape[0]
    slot = lax.broadcasted_iota(jnp.int32, (rows, EXPERTS * CAP), 1)
    parts = [ref[...] for ref in returned_refs]
    parts = jnp.concatenate([part.astype(jnp.float32) for part in parts], axis=0).astype(jnp.bfloat16)
    selector = [(slot == target_ref[:, k : k + 1]).astype(jnp.float32) for k in range(TOP)]
    selector = jnp.concatenate(selector, axis=0).astype(jnp.bfloat16)
    picked = jnp.dot(selector, parts, preferred_element_type=jnp.float32)
    total = jnp.zeros((rows, D), jnp.float32)
    for k in range(TOP):
        total = total + picked[k * rows : (k + 1) * rows] * probs_ref[:, k : k + 1]
    out_ref[...] = (residual_ref[...].astype(jnp.float32) + total).astype(jnp.bfloat16)


def combine(returned, target, probs, residual):
    return pl.pallas_call(
        combine_kernel,
        out_shape=jax.ShapeDtypeStruct(residual.shape, jnp.bfloat16),
        in_specs=[VMEM] * (3 + len(returned)),
        out_specs=VMEM,
        compiler_params=pltpu.CompilerParams(vmem_limit_bytes=24 * MB),
        name="combine",
    )(target, probs, residual, *returned)


def places_of(ids):
    rows = ids.shape[0]
    onehot = (ids[:, :, None] == jnp.arange(EXPERTS, dtype=jnp.int32)).astype(jnp.float32)
    named = jnp.sum(onehot, axis=1)
    earlier = (jnp.arange(rows)[:, None] > jnp.arange(rows)[None, :]).astype(jnp.bfloat16)
    before = jnp.dot(earlier, named.astype(jnp.bfloat16), preferred_element_type=jnp.float32)
    slot = jnp.sum(onehot * before[:, None, :], axis=2).astype(jnp.int32)
    return slot


def shards(
    planes,
    shared,
    hidden_in,
    queries,
    key_proj,
    value_proj,
    tile_mask,
    out_weight,
    moe_gain,
    gate_weight,
    up_weight,
    down_weight,
    expert_ids,
    gate_probs,
):
    ctx = ("plane", "seat")
    world = planes * shared
    plane = lax.axis_index("plane")
    seat = lax.axis_index("seat")
    me = plane * shared + seat
    mine = lax.axis_index("exp") * planes + plane
    place = jnp.stack([plane, seat, mine]).astype(jnp.int32)

    def swap(x, bit):
        return lax.ppermute(x, ctx, [(i, i ^ bit) for i in range(world)])

    def tie(value, places):
        places = [at for at in places if at in pieces]
        value, found = lax.optimization_barrier((value, [pieces[at] for at in places]))
        pieces.update(zip(places, found))
        return value

    ids = expert_ids[0]
    spot = places_of(ids)
    target = ids * CAP + spot
    back = (ids ^ mine) * CAP + spot
    target = target.T
    order = key_order(tile_mask[0], me, world)
    own = jnp.concatenate([key_proj[0], value_proj[0]], axis=1)
    bit = world // 2
    half = shared // 2
    blocks = {0: own, bit: swap(own, bit)}
    packed = pack(place, gate_weight, up_weight, down_weight)
    far = [k for k in range(planes) if k >= planes // 2 and k]
    near = [k for k in range(planes) if k < planes // 2 and k]
    pieces = {(0, 0): packed[0]}
    for k in far[:1] + near:
        pieces[0, k] = swap(packed[k], k * shared)
    pieces[half, 0] = swap(packed[0], half)
    bit //= 2
    while bit:
        if bit == 1:
            last = world - 2
            blocks[last] = tie(blocks[last], [(2, 0)])
            blocks[last], order, target, back = lax.optimization_barrier((blocks[last], order, target, back))
            if far:
                early = half + shared
                blocks[early], second = lax.optimization_barrier((blocks[early], packed[far[1]]))
                pieces[0, far[1]] = swap(second, far[1] * shared)
        blocks.update({m | bit: swap(x, bit) for m, x in list(blocks.items())})
        bit //= 2
    blocks = tie(blocks, [(0, 2)])
    bit = half
    while bit:
        for (m, k), x in list(pieces.items()):
            if (m | bit, k) not in pieces:
                pieces[m | bit, k] = swap(x, bit)
        bit //= 2

    live, where, allowed = order
    attention_out, residual, outgoing = attend(
        live,
        where,
        allowed,
        queries[0],
        target,
        out_weight,
        hidden_in[0],
        moe_gain[None],
        [blocks[m] for m in range(world)],
    )
    outgoing = tie(outgoing, [(2, 2)])
    arrived = lax.all_to_all(
        outgoing.reshape(EXPERTS, CAP, D), ("exp", "plane"), split_axis=0, concat_axis=0, tiled=True
    )
    weights = [pieces[m, k] for m in range(shared) for k in range(planes)]
    first = [j for j in range(EXPERTS) if planes > 1 and j % planes >= planes // 2]
    first += [j for j in range(planes, EXPERTS) if j not in first]
    second = [j for j in range(EXPERTS) if j not in first]
    returned = {}
    for group in (first, second):
        for j, x in zip(group, run_expert(place, arrived, group, weights, planes, shared)):
            step = j % planes * (EXPERTS // planes) + j // planes
            pairs = [(i, i ^ step) for i in range(EXPERTS)]
            returned[j] = lax.ppermute(x, ("plane", "exp"), pairs) if j else x
    layer_out = combine([returned[j] for j in range(EXPERTS)], back, gate_probs[0], residual)
    return attention_out[None], layer_out[None]


def solution(mesh):
    n_ctx, n_exp = mesh.shape["ctx"], mesh.shape["exp"]
    planes = EXPERTS // n_exp
    shared = n_ctx // planes
    fine = Mesh(mesh.devices.reshape(planes, shared, n_exp), ("plane", "seat", "exp"))
    split = P("exp", ("plane", "seat"), None)
    return jax.shard_map(
        functools.partial(shards, planes, shared),
        mesh=fine,
        in_specs=(split, split, split, split, split, P(), P(), split, split, split, split, split),
        out_specs=(split, split),
        check_vma=False,
    )
```

```python
import functools

import jax
import jax.numpy as jnp
from jax import lax
from jax.experimental import pallas as pl
from jax.experimental.pallas import tpu as pltpu
from jax.sharding import Mesh, PartitionSpec as P

D = 1024
HEADS = 8
KV_HEADS = 2
EXPERTS = 8
TOP = 2
TILE = 32
CAP = 72
HEAD = D // HEADS
GROUPS = HEADS // KV_HEADS
KVW = KV_HEADS * HEAD
SLOTS = EXPERTS * CAP
MB = 1 << 20

VMEM = pl.BlockSpec(memory_space=pltpu.VMEM)
SMEM = pl.BlockSpec(memory_space=pltpu.SMEM)
ANY = pl.BlockSpec(memory_space=pl.ANY)


def pack_kernel(planes, place_ref, gate_ref, up_ref, down_ref, *rest):
    outs, sems = rest[:planes], rest[planes]
    plane = place_ref[0]
    copies = []
    for k in range(planes):
        owner = plane ^ k
        for w, ref in enumerate((gate_ref, up_ref, down_ref)):
            copies.append(pltpu.make_async_copy(ref.at[owner], outs[k].at[w], sems.at[3 * k + w]))
    for copy in copies:
        copy.start()
    for copy in copies:
        copy.wait()


def pack(place, gate, up, down):
    planes, rows, ff = gate.shape
    return pl.pallas_call(
        functools.partial(pack_kernel, planes),
        out_shape=[jax.ShapeDtypeStruct((3, rows, ff), gate.dtype)] * planes,
        in_specs=[SMEM, ANY, ANY, ANY],
        out_specs=[VMEM] * planes,
        scratch_shapes=[pltpu.SemaphoreType.DMA((3 * planes,))],
        name="pack_weights",
    )(place, gate, up, down)


def attend_kernel(blocks, live_ref, spot_ref, allowed_ref, query_in, target_ref, out_w_in, hidden_in, gain_ref, *rest):
    kv_in = rest[:blocks]
    attention_ref, residual_ref, outgoing_ref = rest[blocks : blocks + 3]
    query_ref, out_w_ref, hidden_ref, kv, packed, scores, top, total, acc, attended, sems = rest[blocks + 3 :]
    rows = query_ref.shape[0]
    chunk = scores.shape[2]
    tiles = live_ref.shape[0]
    per_chunk = chunk // TILE
    first = [pltpu.make_async_copy(query_in, query_ref, sems.at[0])]
    for i in range(blocks):
        first.append(pltpu.make_async_copy(kv_in[i], kv.at[pl.ds(i * rows, rows)], sems.at[3 + i]))
    late = [
        pltpu.make_async_copy(hidden_in, hidden_ref, sems.at[1]),
        pltpu.make_async_copy(out_w_in, out_w_ref, sems.at[2]),
    ]
    for copy in first + late:
        copy.start()
    for copy in first:
        copy.wait()

    @pl.loop(0, tiles)
    def _(i):
        @pl.when(live_ref[i] > 0)
        def _():
            source = pl.ds(pl.multiple_of(i * TILE, TILE), TILE)
            packed[pl.ds(pl.multiple_of(spot_ref[i] * TILE, TILE), TILE), :] = kv[source, :]

    used = spot_ref[tiles - 1] + live_ref[tiles - 1]
    chunks = (used + per_chunk - 1) // per_chunk

    @pl.loop(used, chunks * per_chunk)
    def _(i):
        packed[pl.ds(pl.multiple_of(i * TILE, TILE), TILE), :] = jnp.zeros((TILE, 2 * KVW), jnp.bfloat16)

    lane_tile = lax.broadcasted_iota(jnp.int32, (128, chunk), 1) // TILE
    widen = (lane_tile == lax.broadcasted_iota(jnp.int32, (128, chunk), 0)).astype(jnp.float32).astype(jnp.bfloat16)
    scale = HEAD ** (-0.5)
    for h in range(KV_HEADS):
        heads = [query_ref[:, (h * GROUPS + g) * HEAD : (h * GROUPS + g + 1) * HEAD] for g in range(GROUPS)]
        query = jnp.concatenate(heads, axis=0)
        top[...] = jnp.full(top.shape, -1e30, jnp.float32)
        total[...] = jnp.zeros(total.shape, jnp.float32)
        acc[...] = jnp.zeros(acc.shape, jnp.float32)

        @pl.loop(0, chunks)
        def _(j):
            keys = packed[pl.ds(pl.multiple_of(j * chunk, 128), chunk), h * HEAD : (h + 1) * HEAD]
            s = lax.dot_general(query, keys, (((1,), (1,)), ((), ())), preferred_element_type=jnp.float32)
            allowed = jnp.dot(allowed_ref[j], widen, preferred_element_type=jnp.float32)
            bias = (allowed - 1.0) * 1e30
            bias = [jnp.broadcast_to(bias[t : t + 1], (TILE, chunk)) for t in range(rows // TILE)]
            bias = jnp.concatenate(bias, axis=0)
            s = s.reshape(GROUPS, rows, chunk) + bias[None]
            s = s.reshape(GROUPS * rows, chunk)
            scores[j] = s
            best = top[...]
            for c in range(0, chunk, 128):
                best = jnp.maximum(best, s[:, c : c + 128])
            top[...] = best

        highest = jnp.max(top[...], axis=1, keepdims=True)
        top[...] = jnp.broadcast_to(highest, top.shape)

        @pl.loop(0, chunks)
        def _(j):
            values = packed[pl.ds(pl.multiple_of(j * chunk, 128), chunk), KVW + h * HEAD : KVW + (h + 1) * HEAD]
            high = top[...]
            s = scores[j]
            parts = []
            running = total[...]
            for c in range(0, chunk, 128):
                w = jnp.exp((s[:, c : c + 128] - high) * scale)
                running = running + w
                parts.append(w.astype(jnp.bfloat16))
            total[...] = running
            weights = jnp.concatenate(parts, axis=1)
            acc[...] += jnp.dot(weights, values, preferred_element_type=jnp.float32)

        denominator = jnp.sum(total[...], axis=1, keepdims=True)
        result = (acc[...] / denominator).astype(jnp.bfloat16)
        for g in range(GROUPS):
            col = (h * GROUPS + g) * HEAD
            attended[:, col : col + HEAD] = result[g * rows : (g + 1) * rows]
    for copy in late:
        copy.wait()
    projected = jnp.dot(attended[...], out_w_ref[...], preferred_element_type=jnp.float32)
    attention_ref[...] = projected.astype(jnp.bfloat16)
    residual = (hidden_ref[...].astype(jnp.float32) + projected).astype(jnp.bfloat16)
    residual_ref[...] = residual
    wide = residual.astype(jnp.float32)
    inverse = lax.rsqrt(jnp.mean(wide * wide, axis=-1, keepdims=True) + 1e-05)
    normed = (wide * inverse * gain_ref[...]).astype(jnp.bfloat16)
    slot = lax.broadcasted_iota(jnp.int32, (SLOTS, rows), 0)
    chosen = (slot == target_ref[0:1, :]) | (slot == target_ref[1:2, :])
    selector = chosen.astype(jnp.float32).astype(jnp.bfloat16)
    outgoing_ref[...] = jnp.dot(selector, normed, preferred_element_type=jnp.float32).astype(jnp.bfloat16)


def attend(live, spot, allowed, query, target, out_w, hidden, gain, blocks):
    rows = query.shape[0]
    chunks = allowed.shape[0]
    n = len(blocks)
    chunk = n * rows // chunks
    return pl.pallas_call(
        functools.partial(attend_kernel, n),
        out_shape=[
            jax.ShapeDtypeStruct((rows, D), jnp.bfloat16),
            jax.ShapeDtypeStruct((rows, D), jnp.bfloat16),
            jax.ShapeDtypeStruct((SLOTS, D), jnp.bfloat16),
        ],
        in_specs=[SMEM, SMEM, VMEM, ANY, VMEM, ANY, ANY, VMEM] + [ANY] * n,
        out_specs=[VMEM] * 3,
        scratch_shapes=[
            pltpu.VMEM((rows, D), jnp.bfloat16),
            pltpu.VMEM((D, D), jnp.bfloat16),
            pltpu.VMEM((rows, D), jnp.bfloat16),
            pltpu.VMEM((n * rows, 2 * KVW), jnp.bfloat16),
            pltpu.VMEM((n * rows, 2 * KVW), jnp.bfloat16),
            pltpu.VMEM((chunks, GROUPS * rows, chunk), jnp.float32),
            pltpu.VMEM((GROUPS * rows, HEAD), jnp.float32),
            pltpu.VMEM((GROUPS * rows, HEAD), jnp.float32),
            pltpu.VMEM((GROUPS * rows, HEAD), jnp.float32),
            pltpu.VMEM((rows, D), jnp.bfloat16),
            pltpu.SemaphoreType.DMA((3 + n,)),
        ],
        compiler_params=pltpu.CompilerParams(vmem_limit_bytes=56 * MB),
        name="attend",
    )(live, spot, allowed, query, target, out_w, hidden, gain, *blocks)


def key_order(tile_mask, me, world):
    tiles, count = tile_mask.shape
    order = me ^ jnp.arange(world)
    mask = jnp.take(tile_mask.reshape(tiles, world, tiles), order, axis=1, mode="clip").reshape(tiles, count)
    mask = (mask > 0).astype(jnp.bfloat16)
    live = jnp.max(mask, axis=0)
    index = jnp.arange(count)
    spot = jnp.dot(live, (index[:, None] < index[None, :]).astype(jnp.bfloat16), preferred_element_type=jnp.float32)
    move = (spot[:, None] == index[None, :].astype(jnp.float32)) & (live[:, None] > 0)
    placed = jnp.dot(mask, move.astype(jnp.bfloat16), preferred_element_type=jnp.float32)
    per_chunk = 2 * tiles
    placed = placed.reshape(tiles, count // per_chunk, per_chunk).transpose(1, 0, 2)
    placed = jnp.pad(placed, ((0, 0), (0, -tiles % 16), (0, 128 - per_chunk))).astype(jnp.bfloat16)
    return live.astype(jnp.int32), spot.astype(jnp.int32), placed


def expert_kernel(planes, shared, cuts, step, group, place_ref, rows_in, *rest):
    count, groups = planes * shared, len(group)
    pieces, out_refs = rest[:count], rest[count : count + groups]
    rows_ref, full, total, sems = rest[count + groups :]
    depth = pieces[0].shape[1]
    plane, seat = place_ref[0], place_ref[1]
    copies = []
    for c, (low, high) in enumerate(cuts):
        for n in range(count):
            m, k = divmod(n, planes)
            at = ((plane ^ k) * shared + (seat ^ m)) * depth
            target = full.at[:, pl.ds(pl.multiple_of(at, depth), depth), pl.ds(low, high - low)]
            copies.append(pltpu.make_async_copy(pieces[n].at[:, :, pl.ds(low, high - low)], target, sems.at[c * count + n]))
            copies[-1].start()
    loaded = [rows_in[place_ref[2] ^ j].astype(jnp.float32) for j in group]
    rows_ref[...] = jnp.concatenate(loaded, axis=0).astype(jnp.bfloat16)
    for c, (low, high) in enumerate(cuts):
        for copy in copies[c * count : (c + 1) * count]:
            copy.wait()
        for at in range(low, high, step):
            rows = rows_ref[...]
            gated = jnp.dot(rows, full[0, :, at : at + step], preferred_element_type=jnp.float32)
            upper = jnp.dot(rows, full[1, :, at : at + step], preferred_element_type=jnp.float32)
            hidden = (gated / (1.0 + jnp.exp(-gated)) * upper).astype(jnp.bfloat16)
            part = lax.dot_general(
                hidden, full[2, :, at : at + step], (((1,), (1,)), ((), ())), preferred_element_type=jnp.float32
            )
            if at == 0:
                total[...] = part
            else:
                total[...] += part
    for g in range(groups):
        out_refs[g][...] = total[g * CAP : (g + 1) * CAP, :].astype(jnp.bfloat16)


def run_expert(place, rows, group, pieces, planes, shared):
    depth, ff = pieces[0].shape[1:]
    count, groups = planes * shared, len(group)
    step = 256
    edges = [0, step, 3 * step, ff]
    cuts = list(zip(edges[:-1], edges[1:]))
    return pl.pallas_call(
        functools.partial(expert_kernel, planes, shared, cuts, step, group),
        out_shape=[jax.ShapeDtypeStruct((CAP, D), jnp.bfloat16)] * groups,
        in_specs=[SMEM, VMEM] + [ANY] * count,
        out_specs=[VMEM] * groups,
        scratch_shapes=[
            pltpu.VMEM((groups * CAP, D), jnp.bfloat16),
            pltpu.VMEM((3, D, ff), jnp.bfloat16),
            pltpu.VMEM((groups * CAP, D), jnp.float32),
            pltpu.SemaphoreType.DMA((count * len(cuts),)),
        ],
        compiler_params=pltpu.CompilerParams(vmem_limit_bytes=56 * MB),
        cost_estimate=pl.CostEstimate(
            flops=6 * groups * CAP * D * ff, bytes_accessed=3 * D * ff * 2, transcendentals=groups * CAP * ff
        ),
        name="expert",
    )(place, rows, *pieces)


def combine_kernel(target_ref, probs_ref, residual_ref, *rest):
    returned_refs, out_ref = rest[:-1], rest[-1]
    rows = residual_ref.shape[0]
    slot = lax.broadcasted_iota(jnp.int32, (rows, EXPERTS * CAP), 1)
    parts = [ref[...] for ref in returned_refs]
    parts = jnp.concatenate([part.astype(jnp.float32) for part in parts], axis=0).astype(jnp.bfloat16)
    selector = [(slot == target_ref[:, k : k + 1]).astype(jnp.float32) for k in range(TOP)]
    selector = jnp.concatenate(selector, axis=0).astype(jnp.bfloat16)
    picked = jnp.dot(selector, parts, preferred_element_type=jnp.float32)
    total = jnp.zeros((rows, D), jnp.float32)
    for k in range(TOP):
        total = total + picked[k * rows : (k + 1) * rows] * probs_ref[:, k : k + 1]
    out_ref[...] = (residual_ref[...].astype(jnp.float32) + total).astype(jnp.bfloat16)


def combine(returned, target, probs, residual):
    return pl.pallas_call(
        combine_kernel,
        out_shape=jax.ShapeDtypeStruct(residual.shape, jnp.bfloat16),
        in_specs=[VMEM] * (3 + len(returned)),
        out_specs=VMEM,
        compiler_params=pltpu.CompilerParams(vmem_limit_bytes=24 * MB),
        name="combine",
    )(target, probs, residual, *returned)


def places_of(ids):
    rows = ids.shape[0]
    onehot = (ids[:, :, None] == jnp.arange(EXPERTS, dtype=jnp.int32)).astype(jnp.float32)
    named = jnp.sum(onehot, axis=1)
    earlier = (jnp.arange(rows)[:, None] > jnp.arange(rows)[None, :]).astype(jnp.bfloat16)
    before = jnp.dot(earlier, named.astype(jnp.bfloat16), preferred_element_type=jnp.float32)
    slot = jnp.sum(onehot * before[:, None, :], axis=2).astype(jnp.int32)
    return slot


def shards(
    planes,
    shared,
    hidden_in,
    queries,
    key_proj,
    value_proj,
    tile_mask,
    out_weight,
    moe_gain,
    gate_weight,
    up_weight,
    down_weight,
    expert_ids,
    gate_probs,
):
    ctx = ("plane", "seat")
    world = planes * shared
    plane = lax.axis_index("plane")
    seat = lax.axis_index("seat")
    me = plane * shared + seat
    mine = lax.axis_index("exp") * planes + plane
    place = jnp.stack([plane, seat, mine]).astype(jnp.int32)

    def swap(x, bit):
        return lax.ppermute(x, ctx, [(i, i ^ bit) for i in range(world)])

    def tie(value, places):
        places = [at for at in places if at in pieces]
        value, found = lax.optimization_barrier((value, [pieces[at] for at in places]))
        pieces.update(zip(places, found))
        return value

    ids = expert_ids[0]
    spot = places_of(ids)
    target = ids * CAP + spot
    back = (ids ^ mine) * CAP + spot
    target = target.T
    order = key_order(tile_mask[0], me, world)
    own = jnp.concatenate([key_proj[0], value_proj[0]], axis=1)
    bit = world // 2
    half = shared // 2
    blocks = {0: own, bit: swap(own, bit)}
    packed = pack(place, gate_weight, up_weight, down_weight)
    far = [k for k in range(planes) if k >= planes // 2 and k]
    near = [k for k in range(planes) if k < planes // 2 and k]
    pieces = {(0, 0): packed[0]}
    for k in far[:1] + near:
        pieces[0, k] = swap(packed[k], k * shared)
    pieces[half, 0] = swap(packed[0], half)
    bit //= 2
    while bit:
        if bit == 1:
            last = world - 2
            blocks[last] = tie(blocks[last], [(2, 0)])
            blocks[last], order, target, back = lax.optimization_barrier((blocks[last], order, target, back))
            if far:
                early = half + shared
                blocks[early], second = lax.optimization_barrier((blocks[early], packed[far[1]]))
                pieces[0, far[1]] = swap(second, far[1] * shared)
        blocks.update({m | bit: swap(x, bit) for m, x in list(blocks.items())})
        bit //= 2
    blocks = tie(blocks, [(0, 2)])
    bit = half
    while bit:
        for (m, k), x in list(pieces.items()):
            if (m | bit, k) not in pieces:
                pieces[m | bit, k] = swap(x, bit)
        bit //= 2

    live, where, allowed = order
    attention_out, residual, outgoing = attend(
        live,
        where,
        allowed,
        queries[0],
        target,
        out_weight,
        hidden_in[0],
        moe_gain[None],
        [blocks[m] for m in range(world)],
    )
    outgoing = tie(outgoing, [(2, 2)])
    arrived = lax.all_to_all(
        outgoing.reshape(EXPERTS, CAP, D), ("exp", "plane"), split_axis=0, concat_axis=0, tiled=True
    )
    weights = [pieces[m, k] for m in range(shared) for k in range(planes)]
    first = [j for j in range(EXPERTS) if planes > 1 and j % planes >= planes // 2]
    first += [j for j in range(planes, EXPERTS) if j not in first]
    second = [j for j in range(EXPERTS) if j not in first]
    returned = {}
    for group in (first, second):
        for j, x in zip(group, run_expert(place, arrived, group, weights, planes, shared)):
            step = j % planes * (EXPERTS // planes) + j // planes
            pairs = [(i, i ^ step) for i in range(EXPERTS)]
            returned[j] = lax.ppermute(x, ("plane", "exp"), pairs) if j else x
    layer_out = combine([returned[j] for j in range(EXPERTS)], back, gate_probs[0], residual)
    return attention_out[None], layer_out[None]


def solution(mesh):
    n_ctx, n_exp = mesh.shape["ctx"], mesh.shape["exp"]
    planes = EXPERTS // n_exp
    shared = n_ctx // planes
    fine = Mesh(mesh.devices.reshape(planes, shared, n_exp), ("plane", "seat", "exp"))
    split = P("exp", ("plane", "seat"), None)
    return jax.shard_map(
        functools.partial(shards, planes, shared),
        mesh=fine,
        in_specs=(split, split, split, split, split, P(), P(), split, split, split, split, split),
        out_specs=(split, split),
        check_vma=False,
    )
```
